128 devices in a mesh: blk: 16 (over x, z_lo, core), grp: 8 (over y, z_hi).
Axes of the slice: x: 4, y: 4, z: 4 (z_hi: 2, z_lo: 2; z = z_hi * 2 + z_lo), core: 2. Of those that a mesh axis runs over, the one named last changes fastest.
Arguments:
- right_vector: bfloat16 [768, 1, 32, 768], P(None, None, 'blk'), may hold values from -10 to 10
- left_vector: bfloat16 [768, 1, 32, 768], P('blk', None, 'grp'), may hold values from -14 to 14
- cycle_weights: bfloat16 [32, 32, 768, 768], P('blk', 'grp'), may hold values from -1 to 4
- screen: int32 [1, 32], replicated, may hold values 0 or 1
Outputs:
- sigma_right: float32 [768, 1, 32, 768], P('blk', None, 'grp')
- sigma_left: float32 [768, 1, 32, 768], P('grp', None, 'blk')
- rayleigh: float32 [1], replicated
The draws below stay inside these ranges and needn't reach their ends.
All inputs are finite; a program needn't handle non-finite values.
Results may differ from the reference program's by a relative error of at most 0.0003.
Values may be sent and summed in bfloat16 or wider, within the bound.
A program may use at most 128 MiB of HBM per device.

```python
import jax
import jax.numpy as jnp
from jax import lax

NV = 768
NI = 1
OCC_DEV = 2
NOCC = 32
N_BLK = 16


def shared_normal(key):
    return jnp.clip(jax.random.normal(key, (NV, NI, NOCC, NV), jnp.float32), -5.0, 5.0)


def occupied_ramp(coefficient):
    steps = jnp.arange(NOCC, dtype=jnp.float32) / max(NOCC - 1, 1)
    return jnp.sqrt(1.0 + coefficient * steps)[None, None, :, None]


def draw_right_vector(key, part):
    field = shared_normal(key) * occupied_ramp(2.0)
    return field.astype(jnp.bfloat16)


def draw_left_vector(key, part):
    common = shared_normal(key)
    key = jax.random.fold_in(key, 11)
    noise = jnp.clip(jax.random.normal(key, (NV, NI, NOCC, NV), jnp.float32), -5.0, 5.0)
    field = (0.8 * common + 0.6 * noise) * occupied_ramp(2.0)
    return field.astype(jnp.bfloat16)


def draw_cycle_weights(key, part):
    key = jax.random.fold_in(key, 23)
    noise_key, diag_key = jax.random.split(key)
    fan = (NOCC * NV) ** (-0.5)
    noise = jnp.clip(jax.random.normal(noise_key, (NOCC, NOCC, NV, NV), jnp.float32), -5.0, 5.0) * fan
    diagonal = jnp.exp(jax.random.uniform(diag_key, (NOCC, NV), jnp.float32, jnp.log(0.5), jnp.log(2.0)))
    same_occ = (jnp.arange(NOCC)[:, None] == jnp.arange(NOCC)[None, :]).astype(jnp.float32)
    same_vir = (jnp.arange(NV)[:, None] == jnp.arange(NV)[None, :]).astype(jnp.float32)
    weights = noise + same_occ[:, :, None, None] * same_vir[None, None, :, :] * diagonal[:, None, :, None]
    return weights.astype(jnp.bfloat16)


def set_ends(drawn, rng, low, top_value):
    dims = drawn.shape
    spot = [jax.random.randint(jax.random.fold_in(rng, axis), (), 0, dims[axis]) for axis in range(len(dims))]
    drawn = drawn.at[tuple(spot)].set(low)
    longest = dims.index(max(dims))
    spot[longest] = (spot[longest] + 1) % dims[longest]
    return drawn.at[tuple(spot)].set(top_value)


def setup_inputs(seed: int = 0) -> dict:
    seeds = jax.random.split(jax.random.key(seed), 5)
    right_vector = draw_right_vector(jax.random.fold_in(seeds[4], 71), 0)
    left_vector = draw_left_vector(jax.random.fold_in(seeds[4], 71), 0)
    cycle_weights = draw_cycle_weights(jax.random.fold_in(seeds[4], 71), 0)
    screen = set_ends((jax.random.randint(seeds[3], (NI, NOCC), 0, 4) < 3).astype(jnp.int32), jax.random.fold_in(seeds[3], 1), 0, 1)
    return {"right_vector": right_vector, "left_vector": left_vector, "cycle_weights": cycle_weights, "screen": screen}


def reference(right_vector, left_vector, cycle_weights, screen):
    left_full = left_vector.astype(jnp.float32)
    screen_mask = screen.astype(jnp.float32)

    def device_step(carried, index):
        first = (index * OCC_DEV).astype(jnp.int32)
        right_slice = lax.dynamic_slice_in_dim(right_vector, first, OCC_DEV, 2).astype(jnp.float32)
        weight_slice = lax.dynamic_slice_in_dim(cycle_weights, first, OCC_DEV, 0).astype(jnp.float32)
        columns = lax.dynamic_slice_in_dim(screen_mask, first, OCC_DEV, 1)
        scaled = right_slice * columns[None, :, :, None]
        carried = carried + jnp.einsum('aime,mjeb->aijb', scaled, weight_slice)
        left_piece = jnp.einsum('aijb,mjeb->aime', left_full, weight_slice) * columns[None, :, :, None]
        return carried, left_piece

    initial = jnp.zeros((NV, NI, NOCC, NV), jnp.float32)
    sigma_right, left_pieces = lax.scan(device_step, initial, jnp.arange(N_BLK, dtype=jnp.int32))
    sigma_left = jnp.transpose(left_pieces, (1, 2, 0, 3, 4)).reshape(NV, NI, NOCC, NV)
    numerator = jnp.sum(left_full * sigma_right)
    denominator = jnp.sum(left_full * right_vector.astype(jnp.float32))
    return sigma_right, sigma_left, (numerator / denominator).reshape(1)
```

```python
import functools

import jax
import jax.numpy as jnp
from jax import lax
from jax.experimental import pallas as pl
from jax.experimental.pallas import tpu as pltpu
from jax.sharding import PartitionSpec as P

MESH = pl.DeviceIdType.MESH
F32 = jnp.float32
BF16 = jnp.bfloat16
I16 = jnp.int16
LEVELS = 32000.0
N_SEM = 96


def dot_nn(a, b):
    return jnp.dot(a, b, preferred_element_type=F32)


def dot_nt(a, b):
    return lax.dot_general(a, b, (((1,), (1,)), ((), ())), preferred_element_type=F32)


def encode(x):
    cols = jnp.max(jnp.abs(x), axis=0, keepdims=True)
    top = functools.reduce(jnp.maximum, [cols[:, i * 128 : (i + 1) * 128] for i in range(6)])
    top = jnp.maximum(top, 1e-30)
    inverse = jnp.concatenate([LEVELS / top] * 6, axis=1)
    return jnp.round(x * inverse).astype(jnp.int32).astype(I16), top * (1.0 / LEVELS)


def decode(q, scale):
    return q.astype(jnp.int32).astype(F32) * jnp.concatenate([scale] * 6, axis=1)


def fold(x):
    rows = functools.reduce(jnp.add, [x[i * 8 : (i + 1) * 8] for i in range(6)])
    return functools.reduce(jnp.add, [rows[:, i * 128 : (i + 1) * 128] for i in range(6)])


def kernel(
    screen_ref, right_hbm, left_hbm, weights_hbm, sr_out, sl_out, ray_out,
    w, r, rs, lg, part, tot, sl,
    zb_s, zb_r, zbs_s, zbs_r,
    ring_s, ring_r, rsc_s, rsc_r,
    zf_s, zf_r, zfs_s, zfs_r,
    ys, yr, yss, ysr,
    hs, hr, hss, hsr,
    sums, xs, ysum,
    load_sem, send_sem, recv_sem, ysend_sem, yrecv_sem,
):
    blk = lax.axis_index("blk")
    grp = lax.axis_index("grp")
    x, zl, c = blk // 4, (blk // 2) % 2, blk % 2
    y, zh = grp // 2, grp % 2
    zo = 1 - zl
    sibling = (blk + 1 - 2 * c, grp)
    z_dev = (blk + 2 - 4 * zl, grp)
    xp_dev = ((blk + 4) % 16, grp)
    xm_dev = ((blk + 12) % 16, grp)
    x2_dev = ((blk + 8) % 16, grp)
    y_devs = [(blk, (grp + 2 * k) % 8) for k in (1, 2, 3)]
    h_dev = (blk, grp + 1 - 2 * zh)

    loads = []

    def load(src, dst):
        copy = pltpu.make_async_copy(src, dst, load_sem.at[len(loads)])
        copy.start()
        loads.append(copy)
        return copy

    def pos(dx, z, core):
        return ((x + dx) % 4) * 4 + z * 2 + core

    here = pos(0, zl, c)
    left_in = load(left_hbm, lg.at[here])
    right_in = load(right_hbm, r)
    weights_in = [[load(weights_hbm.at[m, j], w.at[m, j]) for m in range(2)] for j in range(4)]

    barrier = pltpu.get_barrier_semaphore()
    partners = [sibling, z_dev, xp_dev, xm_dev, x2_dev, h_dev] + y_devs
    for partner in partners:
        pl.semaphore_signal(barrier, inc=1, device_id=partner, device_id_type=MESH)
    pl.semaphore_wait(barrier, len(partners))

    started = []

    def send(src, dst, device):
        k = len(started)
        copy = pltpu.make_async_remote_copy(
            src_ref=src, dst_ref=dst, send_sem=send_sem.at[k], recv_sem=recv_sem.at[k],
            device_id=device, device_id_type=MESH,
        )
        copy.start()
        started.append(copy)
        return copy

    def hand(p, device, js=None):
        ref = lg.at[p] if js is None else lg.at[p, pl.ds(js, 2)]
        return send(ref, ref, device)

    left_in.wait()
    got_xp = hand(here, xp_dev)
    got_xm = hand(here, xm_dev)
    got_z = hand(here, z_dev)
    sib_got = [hand(here, sibling)]

    def right_part(j):
        for copy in weights_in[j]:
            copy.wait()
        acc = dot_nn(rs[0].reshape(768, 768), w[0, j]) + dot_nn(rs[1].reshape(768, 768), w[1, j])
        part[j] = acc.reshape(8, 2, 48, 768)
        return send(part.at[j, :, 1 - c], tot.at[j], sibling)

    def join(j, copy):
        copy.wait_recv()

        def step(k, carry):
            tot[j, k] = tot[j, k] + part[j, k, c]
            return carry

        lax.fori_loop(0, 8, step, 0)

    right_in.wait()
    for m in range(2):
        keep = screen_ref[0, 2 * blk + m].astype(F32).astype(BF16)

        def screen_rows(k, carry, m=m, keep=keep):
            rs[m, k] = r[m, k] * keep
            return carry

        lax.fori_loop(0, 16, screen_rows, 0)
    joined = [right_part(0), right_part(1)]

    zb_got = []
    for j in range(2):
        join(j, joined[j])
        for k in range(4):
            q, scale = encode(tot[j, k * 2 + zo])
            zb_s[j, k] = q
            zbs_s[j, k : k + 1] = scale
        zb_got.append(send(zb_s.at[j], zb_r.at[j], z_dev))
        zb_got.append(send(zbs_s.at[j], zbs_r.at[j], z_dev))

    got_xp.wait_recv()
    fwd_p = hand(pos(-1, zl, c), xp_dev, 0)
    got_xm.wait_recv()
    fwd_m = hand(pos(1, zl, c), xm_dev, 2)
    got_z.wait_recv()
    zgot_xp = hand(pos(0, zo, c), xp_dev)
    zgot_xm = hand(pos(0, zo, c), xm_dev)
    sib_got.append(hand(pos(0, zo, c), sibling))
    sib_near = [hand(pos(-1, zl, c), sibling), hand(pos(1, zl, c), sibling)]

    joined += [right_part(2), right_part(3)]

    sums[0:2] = jnp.zeros((2, 8, 128), F32)
    y_sent = []

    def left_part(chunks):
        rows = [pos(dx, z, core) for dx, z in chunks for core in range(2)]
        for m in range(2):
            acc = None
            for j in range(4):
                block = jnp.concatenate([lg[p, j] for p in rows], axis=0)
                term = dot_nt(block, w[m, j])
                acc = term if acc is None else acc + term
            for i, p in enumerate(rows):
                dx, z = chunks[i // 2]
                slab = acc[i * 48 : (i + 1) * 48]
                sl[dx % 4, z, m, i % 2] = slab
                sums[0] += fold(slab * rs[m, p].astype(F32))
        for dx, z in chunks:
            for m in range(2):
                for core in range(2):
                    q, scale = encode(sl[dx % 4, z, m, core])
                    ys[dx % 4, z, m, core] = q
                    yss[dx % 4, z, m * 2 + core : m * 2 + core + 1] = scale
            owner = (x + dx) % 4
            step = (y + 4 - owner) % 4
            slot = (step + 3) % 4

            def go(dx=dx, z=z, owner=owner, slot=slot):
                for copy in y_copies(dx % 4, z, slot, (blk, owner * 2 + zh)):
                    copy.start()

            pl.when(step != 0)(go)
            y_sent.append((dx % 4, z, step, slot, owner))

    def y_copies(d, z, slot, device):
        return [
            pltpu.make_async_remote_copy(
                src_ref=ys.at[d, z], dst_ref=yr.at[slot, z],
                send_sem=ysend_sem.at[d, z, 0], recv_sem=yrecv_sem.at[slot, z, 0],
                device_id=device, device_id_type=MESH,
            ),
            pltpu.make_async_remote_copy(
                src_ref=yss.at[d, z], dst_ref=ysr.at[slot, z],
                send_sem=ysend_sem.at[d, z, 1], recv_sem=yrecv_sem.at[slot, z, 1],
                device_id=device, device_id_type=MESH,
            ),
        ]

    for copy in sib_got:
        copy.wait_recv()
    left_part([(0, zl), (0, zo)])

    fwd_p.wait_recv()
    fwd_m.wait_recv()
    sib_near.append(hand(pos(2, zl, c), sibling))
    for j in (2, 3):
        join(j, joined[j])
    for copy in sib_near:
        copy.wait_recv()
    left_part([(1, zl), (-1, zl), (2, zl)])

    zgot_xp.wait_recv()
    zfwd_p = hand(pos(-1, zo, c), xp_dev, 0)
    zgot_xm.wait_recv()
    zfwd_m = hand(pos(1, zo, c), xm_dev, 2)
    sib_far = [hand(pos(-1, zo, c), sibling), hand(pos(1, zo, c), sibling)]

    def ring_send(n, kind, block, device):
        q, scale = encode(block)
        ring_s[n, kind] = q
        rsc_s[n, kind, 0:1] = scale
        return [
            send(ring_s.at[n, kind], ring_r.at[n, kind], device),
            send(rsc_s.at[n, kind], rsc_r.at[n, kind], device),
        ]

    def ring_take(n, kind, copies):
        for copy in copies:
            copy.wait_recv()
        return decode(ring_r[n, kind], rsc_r[n, kind, 0:1])

    def xz(dx, z):
        return ((x + dx) % 4) * 2 + z

    def ring_first(n, ja, jb, z):
        hop_p = ring_send(n, 0, tot[ja, xz(2, z)], xp_dev)
        hop_m = ring_send(n, 1, tot[jb, xz(2, z)], xm_dev)
        dir_p = ring_send(n, 2, tot[jb, xz(1, z)], xp_dev)
        dir_m = ring_send(n, 3, tot[ja, xz(-1, z)], xm_dev)
        return hop_p, hop_m, dir_p, dir_m

    def ring_second(n, ja, jb, z, first):
        acc_p = ring_send(n, 4, tot[ja, xz(1, z)] + ring_take(n, 0, first[0]), xp_dev)
        acc_m = ring_send(n, 5, tot[jb, xz(-1, z)] + ring_take(n, 1, first[1]), xm_dev)
        return acc_p, acc_m

    def ring_third(n, ja, jb, z, first, second):
        at = xz(0, z)
        tot[ja, at] = tot[ja, at] + ring_take(n, 3, first[3]) + ring_take(n, 4, second[0])
        tot[jb, at] = tot[jb, at] + ring_take(n, 2, first[2]) + ring_take(n, 5, second[1])

    first0 = ring_first(0, 2, 3, zo)
    first1 = ring_first(1, 2, 3, zl)
    for copy in zb_got:
        copy.wait_recv()
    for j in range(2):
        for k in range(4):
            at = k * 2 + zl
            tot[j, at] = tot[j, at] + decode(zb_r[j, k], zbs_r[j, k : k + 1])
    first2 = ring_first(2, 0, 1, zl)

    zfwd_p.wait_recv()
    zfwd_m.wait_recv()
    sib_far.append(hand(pos(2, zo, c), sibling))
    for copy in sib_far:
        copy.wait_recv()
    left_part([(1, zo), (-1, zo), (2, zo)])

    def pairs():
        for m in range(2):
            def step(p, acc, m=m):
                return acc + fold(lg[p, 2 * c + m].astype(F32) * r[m, p].astype(F32))

            sums[1] += lax.fori_loop(0, 16, step, jnp.zeros((8, 128), F32))

    pl.when(blk // 2 == grp)(pairs)

    second0 = ring_second(0, 2, 3, zo, first0)
    sum_copy = send(sums.at[pl.ds(0, 2)], sums.at[pl.ds(2, 2)], sibling)
    second1 = ring_second(1, 2, 3, zl, first1)
    second2 = ring_second(2, 0, 1, zl, first2)

    sum_copy.wait_recv()
    sums[4:6] = sums[0:2] + sums[2:4]
    sum_copy = send(sums.at[pl.ds(4, 2)], sums.at[pl.ds(6, 2)], z_dev)

    ring_third(0, 2, 3, zo, first0, second0)
    for i, j in enumerate((2, 3)):
        q, scale = encode(tot[j, xz(0, zo)])
        zf_s[i] = q
        zfs_s[i : i + 1] = scale
    zf_got = [send(zf_s, zf_r, z_dev), send(zfs_s, zfs_r, z_dev)]

    sum_copy.wait_recv()
    sums[8:10] = sums[4:6] + sums[6:8]
    sum_copy = send(sums.at[pl.ds(8, 2)], sums.at[pl.ds(10, 2)], h_dev)

    own = (y + 4 - x) % 4
    for k in range(3):
        for z in range(2):
            for copy in y_copies(0, z, k, y_devs[0]):
                copy.wait_recv()

    def y_total(z, m, core):
        total = sl[own, z, m, core]
        for k in range(3):
            at = pl.ds(m * 2 + core, 1)
            total = total + decode(yr[k, z, m, core], ysr[k, z, at])
        return total

    for m in range(2):
        for core in range(2):
            q, scale = encode(y_total(1 - zh, m, core))
            hs[m, core] = q
            hss[m * 2 + core : m * 2 + core + 1] = scale
    h_got = [send(hs, hr, h_dev), send(hss, hsr, h_dev)]

    sum_copy.wait_recv()
    xs[x] = sums[8:10] + sums[10:12]
    x_sums = [send(xs.at[x], xs.at[x], device) for device in (xp_dev, xm_dev, x2_dev)]

    ring_third(1, 2, 3, zl, first1, second1)
    ring_third(2, 0, 1, zl, first2, second2)
    sr_out[0] = tot[0, xz(0, zl)]
    sr_out[1] = tot[1, xz(0, zl)]

    for copy in x_sums:
        copy.wait_recv()
    ysum[y] = xs[0] + xs[1] + xs[2] + xs[3]
    y_sums = [send(ysum.at[y], ysum.at[y], device) for device in y_devs]

    for copy in zf_got:
        copy.wait_recv()
    for i, j in enumerate((2, 3)):
        sr_out[j] = tot[j, xz(0, zl)] + decode(zf_r[i], zfs_r[i : i + 1])

    for copy in h_got:
        copy.wait_recv()
    for m in range(2):
        keep = screen_ref[0, 2 * blk + m].astype(F32)
        for core in range(2):
            at = m * 2 + core
            total = y_total(zh, m, core) + decode(hr[m, core], hsr[at : at + 1])
            sl_out[m, core] = total * keep

    for copy in y_sums:
        copy.wait_recv()
    both = ysum[0] + ysum[1] + ysum[2] + ysum[3]
    numerator = jnp.sum(jnp.sum(both[0], axis=0, keepdims=True), axis=1, keepdims=True)
    denominator = jnp.sum(jnp.sum(both[1], axis=0, keepdims=True), axis=1, keepdims=True)
    ray_out[...] = jnp.broadcast_to(numerator / denominator, (8, 128))

    for copy in started:
        copy.wait_send()
    for d, z, step, slot, owner in y_sent:

        def done(d=d, z=z, slot=slot, owner=owner):
            for copy in y_copies(d, z, slot, (blk, owner * 2 + zh)):
                copy.wait_send()

        pl.when(step != 0)(done)


def body(right_vector, left_vector, cycle_weights, screen):
    right = right_vector.reshape(16, 48, 2, 768).transpose(2, 0, 1, 3)
    left = left_vector.reshape(48, 4, 768).transpose(1, 0, 2)
    anywhere = pl.BlockSpec(memory_space=pl.ANY)
    vmem = pl.BlockSpec(memory_space=pltpu.VMEM)
    scratch = [
        pltpu.VMEM((2, 4, 768, 768), BF16),
        pltpu.VMEM((2, 16, 48, 768), BF16),
        pltpu.VMEM((2, 16, 48, 768), BF16),
        pltpu.VMEM((16, 4, 48, 768), BF16),
        pltpu.VMEM((4, 8, 2, 48, 768), F32),
        pltpu.VMEM((4, 8, 48, 768), F32),
        pltpu.VMEM((4, 2, 2, 2, 48, 768), F32),
        pltpu.VMEM((2, 4, 48, 768), I16),
        pltpu.VMEM((2, 4, 48, 768), I16),
        pltpu.VMEM((2, 8, 128), F32),
        pltpu.VMEM((2, 8, 128), F32),
        pltpu.VMEM((3, 6, 48, 768), I16),
        pltpu.VMEM((3, 6, 48, 768), I16),
        pltpu.VMEM((3, 6, 8, 128), F32),
        pltpu.VMEM((3, 6, 8, 128), F32),
        pltpu.VMEM((2, 48, 768), I16),
        pltpu.VMEM((2, 48, 768), I16),
        pltpu.VMEM((8, 128), F32),
        pltpu.VMEM((8, 128), F32),
        pltpu.VMEM((4, 2, 2, 2, 48, 768), I16),
        pltpu.VMEM((3, 2, 2, 2, 48, 768), I16),
        pltpu.VMEM((4, 2, 8, 128), F32),
        pltpu.VMEM((3, 2, 8, 128), F32),
        pltpu.VMEM((2, 2, 48, 768), I16),
        pltpu.VMEM((2, 2, 48, 768), I16),
        pltpu.VMEM((8, 128), F32),
        pltpu.VMEM((8, 128), F32),
        pltpu.VMEM((12, 8, 128), F32),
        pltpu.VMEM((4, 2, 8, 128), F32),
        pltpu.VMEM((4, 2, 8, 128), F32),
        pltpu.SemaphoreType.DMA((10,)),
        pltpu.SemaphoreType.DMA((N_SEM,)),
        pltpu.SemaphoreType.DMA((N_SEM,)),
        pltpu.SemaphoreType.DMA((4, 2, 2)),
        pltpu.SemaphoreType.DMA((3, 2, 2)),
    ]
    sr, sl, ray = pl.pallas_call(
        kernel,
        out_shape=(
            jax.ShapeDtypeStruct((4, 48, 768), F32),
            jax.ShapeDtypeStruct((2, 2, 48, 768), F32),
            jax.ShapeDtypeStruct((8, 128), F32),
        ),
        in_specs=[pl.BlockSpec(memory_space=pltpu.SMEM), anywhere, anywhere, anywhere],
        out_specs=(vmem, vmem, vmem),
        scratch_shapes=scratch,
        compiler_params=pltpu.CompilerParams(
            collective_id=0, has_side_effects=True, vmem_limit_bytes=60 * 2**20
        ),
        cost_estimate=pl.CostEstimate(
            flops=14_500_000_000, bytes_accessed=13_000_000, transcendentals=0
        ),
    )(screen, right, left, cycle_weights)
    sigma_right = sr.transpose(1, 0, 2)[:, None]
    sigma_left = sl.reshape(2, 96, 768).transpose(1, 0, 2)[:, None]
    return sigma_right, sigma_left, ray[0, :1]


def solution(mesh):
    in_specs = (
        P(None, None, "blk", None),
        P("blk", None, "grp", None),
        P("blk", "grp", None, None),
        P(),
    )
    out_specs = (P("blk", None, "grp", None), P("grp", None, "blk", None), P())
    return jax.shard_map(body, mesh=mesh, in_specs=in_specs, out_specs=out_specs, check_vma=False)
```

```python
import functools

import jax
import jax.numpy as jnp
from jax import lax
from jax.experimental import pallas as pl
from jax.experimental.pallas import tpu as pltpu
from jax.sharding import PartitionSpec as P

MESH = pl.DeviceIdType.MESH
F32 = jnp.float32
BF16 = jnp.bfloat16
I16 = jnp.int16
LEVELS = 32000.0
N_SEM = 120


def dot_nn(a, b):
    return jnp.dot(a, b, preferred_element_type=F32)


def dot_nt(a, b):
    return lax.dot_general(a, b, (((1,), (1,)), ((), ())), preferred_element_type=F32)


def wide(scale):
    return jnp.concatenate([scale] * 6, axis=1)


def band(i):
    return pl.ds(pl.multiple_of(i * 16, 16), 16)


def encode(src, q_ref, scale_ref):
    def top_step(i, top):
        return jnp.maximum(top, jnp.abs(src[band(i)]))

    top = lax.fori_loop(0, 3, top_step, jnp.full((16, 768), 1e-30, F32))
    top = jnp.max(top, axis=0, keepdims=True)
    top = functools.reduce(jnp.maximum, [top[:, i * 128 : (i + 1) * 128] for i in range(6)])
    inverse = wide(LEVELS / top)
    scale_ref[...] = jnp.broadcast_to(top * (1.0 / LEVELS), (8, 128))

    def step(i, carry):
        q_ref[band(i)] = jnp.round(src[band(i)] * inverse).astype(jnp.int32).astype(I16)
        return carry

    lax.fori_loop(0, 3, step, 0)


def decode_add(dst, src, terms, factor=1.0):
    scales = [wide(scale[0:1]) for _, scale in terms]

    def step(i, carry):
        total = src[band(i)]
        for (q, _), scale in zip(terms, scales):
            total = total + q[band(i)].astype(jnp.int32).astype(F32) * scale
        dst[band(i)] = total * factor
        return carry

    lax.fori_loop(0, 3, step, 0)


def fold(x):
    rows = functools.reduce(jnp.add, [x[i * 8 : (i + 1) * 8] for i in range(6)])
    return functools.reduce(jnp.add, [rows[:, i * 128 : (i + 1) * 128] for i in range(6)])


def kernel(
    screen_ref, right_hbm, left_hbm, weights_hbm, sr_out, sl_out, ray_out,
    w, right_raw, left_raw, r, rs, lg, part, tot, sl,
    ring_s, ring_r, rsc_s, rsc_r,
    zf_s, zf_r, zfs_s, zfs_r,
    ys, yr, yh, yss, ysr, yhs,
    hs, hr, hss, hsr,
    sums, xs, ysum, ray,
    load_sem, send_sem, recv_sem, ysend_sem, yrecv_sem, yhop_sem, part_sem,
):
    blk = lax.axis_index("blk")
    grp = lax.axis_index("grp")
    x, zl, c = blk // 4, (blk // 2) % 2, blk % 2
    y, zh = grp // 2, grp % 2
    zo = 1 - zl
    sibling = (blk + 1 - 2 * c, grp)
    z_dev = (blk + 2 - 4 * zl, grp)
    xp_dev = ((blk + 4) % 16, grp)
    xm_dev = ((blk + 12) % 16, grp)
    x2_dev = ((blk + 8) % 16, grp)
    y_devs = [(blk, (grp + 2 * k) % 8) for k in (1, 2, 3)]
    h_dev = (blk, grp + 1 - 2 * zh)

    loads = []

    def load(src, dst):
        copy = pltpu.make_async_copy(src, dst, load_sem.at[len(loads)])
        copy.start()
        loads.append(copy)
        return copy

    def pos(dx, z, core):
        return ((x + dx) % 4) * 4 + z * 2 + core

    here = pos(0, zl, c)
    left_in = load(left_hbm, left_raw)
    right_in = load(right_hbm, right_raw)

    def weight_copy(j, m):
        return pltpu.make_async_copy(weights_hbm.at[m, j], w.at[m, j], load_sem.at[2 + j * 2 + m])

    for j in range(4):
        for m in range(2):
            weight_copy(j, m).start()

    barrier = pltpu.get_barrier_semaphore()
    partners = [sibling, z_dev, xp_dev, xm_dev, x2_dev, h_dev] + y_devs
    for partner in partners:
        pl.semaphore_signal(barrier, inc=1, device_id=partner, device_id_type=MESH)
    left_in.wait()
    for j in range(4):
        lg[here, j] = left_raw[:, j, :]
    pl.semaphore_wait(barrier, len(partners))

    started = []

    def send(src, dst, device):
        k = len(started)
        copy = pltpu.make_async_remote_copy(
            src_ref=src, dst_ref=dst, send_sem=send_sem.at[k], recv_sem=recv_sem.at[k],
            device_id=device, device_id_type=MESH,
        )
        copy.start()
        started.append(copy)
        return copy

    def hand(p, device, j=0, count=4):
        ref = lg.at[p, pl.ds(j, count)]
        return send(ref, ref, device)

    def await_all(copies):
        for copy in copies:
            copy.wait_recv()

    own_xp = [hand(here, xp_dev, 0, 2), hand(here, xp_dev, 2, 2)]
    own_xm = [hand(here, xm_dev, 2, 2), hand(here, xm_dev, 0, 2)]
    own_z = [hand(here, z_dev, 0, 2), hand(here, z_dev, 2, 2)]
    sib_0 = [hand(here, sibling)]
    sib_1 = []

    def part_copy(j):
        return pltpu.make_async_remote_copy(
            src_ref=part.at[j, :, 1 - c], dst_ref=tot.at[j], send_sem=part_sem.at[j, 0],
            recv_sem=part_sem.at[j, 1], device_id=sibling, device_id_type=MESH,
        )

    def right_parts(first, last):
        def step(j, carry):
            acc = dot_nn(rs[0].reshape(768, 768), w[0, j]) + dot_nn(rs[1].reshape(768, 768), w[1, j])
            part[j] = acc.reshape(8, 2, 48, 768)
            part_copy(j).start()
            return carry

        lax.fori_loop(first, last, step, 0)

    def join_parts(first):
        for j in range(first, first + 2):
            part_copy(j).wait_recv()

        def step(k, carry):
            j, at = first + k // 8, k % 8
            tot[j, at] = tot[j, at] + part[j, at, c]
            return carry

        lax.fori_loop(0, 16, step, 0)

    sums[0:2] = jnp.zeros((2, 8, 128), F32)

    def left_rows(chunks, m):
        rows = [pos(dx, z, core) for dx, z in chunks for core in range(2)]
        acc = None
        for j in range(4):
            block = jnp.concatenate([lg[p, j] for p in rows], axis=0)
            term = dot_nt(block, w[m, j])
            acc = term if acc is None else acc + term
        for i in range(len(rows)):
            dx, z = chunks[i // 2]
            sl[dx % 4, z, m, i % 2] = acc[i * 48 : (i + 1) * 48]

    def left_both(chunks):
        def step(m, carry):
            left_rows(chunks, m)
            return carry

        lax.fori_loop(0, 2, step, 0)

    def correlate(chunks):
        for dx, z in chunks:

            def step(k, acc, dx=dx, z=z):
                m, core = k // 2, k % 2
                return acc + fold(sl[dx % 4, z, m, core] * rs[m, pos(dx, z, core)].astype(F32))

            sums[0] += lax.fori_loop(0, 4, step, jnp.zeros((8, 128), F32))

    def role(dx):
        owner = (x + dx) % 4
        step = (y + 4 - owner) % 4
        return owner, step, step // 2

    def y_copies(dx, z, m, dst, dst_scale, sems, device):
        return [
            pltpu.make_async_remote_copy(
                src_ref=ys.at[dx % 4, z, m], dst_ref=dst, send_sem=ysend_sem.at[dx % 4, z, m, 0],
                recv_sem=sems.at[0], device_id=device, device_id_type=MESH,
            ),
            pltpu.make_async_remote_copy(
                src_ref=yss.at[dx % 4, z, m], dst_ref=dst_scale, send_sem=ysend_sem.at[dx % 4, z, m, 1],
                recv_sem=sems.at[1], device_id=device, device_id_type=MESH,
            ),
        ]

    def to_owner(dx, z, m, side, device):
        return y_copies(dx, z, m, yr.at[side, z, m], ysr.at[side, z, m], yrecv_sem.at[side, z, m], device)

    def to_side(dx, z, m, device):
        return y_copies(dx, z, m, yh.at[z, m], yhs.at[z, m], yhop_sem.at[z, m], device)

    def y_encode(d, z, m):
        def step(core, carry):
            encode(sl.at[d, z, m, core], ys.at[d, z, m, core], yss.at[d, z, m, core])
            return carry

        lax.fori_loop(0, 2, step, 0)

    def y_far(dx, z):
        owner, step, side = role(dx)
        d = dx % 4

        def far():
            for m in range(2):
                y_encode(d, z, m)
                for copy in to_side(dx, z, m, y_devs[2 * m]):
                    copy.start()

        pl.when(step == 2)(far)

    def y_near(dx, z):
        owner, step, side = role(dx)
        d = dx % 4

        def near():
            y_encode(d, z, side)
            for copy in to_owner(dx, z, side, side, (blk, owner * 2 + zh)):
                copy.start()

        pl.when(step % 2 == 1)(near)

    def y_second(dx, z):
        owner, step, side = role(dx)
        d = dx % 4
        other = 1 - side

        def near():
            for copy in to_side(dx, z, other, y_devs[0]):
                copy.wait_recv()

            def add(core, carry):
                at = sl.at[d, z, other, core]
                decode_add(at, at, [(yh.at[z, other, core], yhs.at[z, other, core])])
                return carry

            lax.fori_loop(0, 2, add, 0)
            y_encode(d, z, other)
            for copy in to_owner(dx, z, other, side, (blk, owner * 2 + zh)):
                copy.start()

        pl.when(step % 2 == 1)(near)

    def y_drain(dx, z):
        owner, step, side = role(dx)

        def done():
            for m in range(2):
                for copy in to_side(dx, z, m, y_devs[0]):
                    copy.wait_send()

        pl.when(step != 0)(done)

    def first_of(chunks):
        for dx, z in chunks:
            y_far(dx, z)
        for dx, z in chunks:
            y_near(dx, z)

    def second_of(chunks):
        for dx, z in chunks:
            y_second(dx, z)

    def ring_send(n, kind, block, device):
        encode(block, ring_s.at[n, kind], rsc_s.at[n, kind])
        return [
            send(ring_s.at[n, kind], ring_r.at[n, kind], device),
            send(rsc_s.at[n, kind], rsc_r.at[n, kind], device),
        ]

    def ring_add(n, at, kinds):
        for _, copies in kinds:
            await_all(copies)
        decode_add(at, at, [(ring_r.at[n, kind], rsc_r.at[n, kind]) for kind, _ in kinds])

    def xz(dx, z):
        return ((x + dx) % 4) * 2 + z

    def ring_hop(n, ja, jb, z):
        hop_p = ring_send(n, 0, tot.at[ja, xz(2, z)], xp_dev)
        hop_m = ring_send(n, 1, tot.at[jb, xz(2, z)], xm_dev)
        return hop_p, hop_m

    def ring_direct(n, ja, jb, z):
        dir_p = ring_send(n, 2, tot.at[jb, xz(1, z)], xp_dev)
        dir_m = ring_send(n, 3, tot.at[ja, xz(-1, z)], xm_dev)
        return dir_p, dir_m

    def ring_second(n, ja, jb, z, hop):
        to_p, to_m = tot.at[ja, xz(1, z)], tot.at[jb, xz(-1, z)]
        ring_add(n, to_p, [(0, hop[0])])
        acc_p = ring_send(n, 4, to_p, xp_dev)
        ring_add(n, to_m, [(1, hop[1])])
        acc_m = ring_send(n, 5, to_m, xm_dev)
        return acc_p, acc_m

    def ring_third(n, ja, jb, z, direct, second):
        at = xz(0, z)
        ring_add(n, tot.at[ja, at], [(3, direct[1]), (4, second[0])])
        ring_add(n, tot.at[jb, at], [(2, direct[0]), (5, second[1])])

    def z_send(n, ja, jb):
        for i, j in enumerate((ja, jb)):
            encode(tot.at[j, xz(0, zo)], zf_s.at[n, i], zfs_s.at[n, i])
        return [send(zf_s.at[n], zf_r.at[n], z_dev), send(zfs_s.at[n], zfs_r.at[n], z_dev)]

    def z_take(n, ja, jb, copies):
        await_all(copies)
        for i, j in enumerate((ja, jb)):
            at = tot.at[j, xz(0, zl)]
            decode_add(at, at, [(zf_r.at[n, i], zfs_r.at[n, i])])

    right_in.wait()
    for m in range(2):

        def right_rows(k, carry, m=m):
            r[m, k] = right_raw[pl.ds(pl.multiple_of(k * 48, 48), 48), m, :]
            return carry

        lax.fori_loop(0, 16, right_rows, 0)

    own_z[0].wait_recv()
    z_xp = hand(pos(0, zo, c), xp_dev, 0, 2)
    own_xp[0].wait_recv()
    far_xp = hand(pos(-1, zl, c), xp_dev, 0, 2)
    own_xm[0].wait_recv()
    far_xm = hand(pos(1, zl, c), xm_dev, 2, 2)
    z_xm1 = hand(pos(0, zo, c), xm_dev, 1, 1)
    z_xm0 = hand(pos(0, zo, c), xm_dev, 0, 1)
    x_z1 = hand(pos(1, zl, c), z_dev, 2, 2)
    sib_1 += [hand(pos(0, zo, c), sibling, 0, 2), hand(pos(-1, zl, c), sibling, 0, 2)]
    sib_1 += [hand(pos(1, zl, c), sibling, 2, 2)]

    for m in range(2):
        keep = screen_ref[0, 2 * blk + m].astype(F32).astype(BF16)

        def screen_rows(k, carry, m=m, keep=keep):
            rs[m, k] = r[m, k] * keep
            return carry

        lax.fori_loop(0, 16, screen_rows, 0)
    for j in (0, 1):
        for m in range(2):
            weight_copy(j, m).wait()
    right_parts(0, 2)

    own_xp[1].wait_recv()
    x_z2 = hand(pos(-1, zl, c), z_dev, 2, 2)
    own_xm[1].wait_recv()
    own_z[1].wait_recv()
    sib_1 += [hand(pos(0, zo, c), sibling, 2, 2), hand(pos(-1, zl, c), sibling, 2, 2)]
    sib_1 += [hand(pos(1, zl, c), sibling, 0, 2)]

    for j in (2, 3):
        for m in range(2):
            weight_copy(j, m).wait()
    right_parts(2, 4)
    join_parts(0)

    far_xm.wait_recv()
    x_z3 = hand(pos(2, zl, c), z_dev, 2, 2)
    z_xp.wait_recv()
    zfar_xp = hand(pos(-1, zo, c), xp_dev, 0, 1)
    z_xm1.wait_recv()
    zfar_xm = hand(pos(1, zo, c), xm_dev, 1, 1)
    x_z1.wait_recv()
    sib_2 = [hand(pos(-1, zo, c), sibling, 0, 2), hand(pos(1, zo, c), sibling, 2, 2)]
    hop0 = ring_hop(0, 0, 1, zo)
    dir0 = ring_direct(0, 0, 1, zo)

    group0 = [(0, 1 - zh), (0, zh)]
    await_all(sib_0)
    await_all(sib_1)
    left_both(group0)

    far_xp.wait_recv()
    sib_far = hand(pos(2, zl, c), sibling)
    z_xm0.wait_recv()
    x_z2.wait_recv()
    sib_2 += [hand(pos(1, zo, c), sibling, 0, 2), hand(pos(-1, zo, c), sibling, 2, 2)]

    first_of(group0)
    join_parts(2)
    hop2 = ring_hop(2, 2, 3, zo)
    dir2 = ring_direct(2, 2, 3, zo)
    hop1 = ring_hop(1, 0, 1, zl)
    hop3 = ring_hop(3, 2, 3, zl)

    zfar_xp.wait_recv()
    zfar_xm.wait_recv()
    x_z3.wait_recv()
    sib_2.append(hand(pos(2, zo, c), sibling))

    group1 = [(1, zl), (-1, zl), (2, zl)]
    sib_far.wait_recv()
    left_both(group1)
    first_of(group1)
    acc0 = ring_second(0, 0, 1, zo, hop0)
    acc2 = ring_second(2, 2, 3, zo, hop2)
    dir1 = ring_direct(1, 0, 1, zl)
    dir3 = ring_direct(3, 2, 3, zl)

    group2 = [(2, zo), (1, zo), (-1, zo)]
    await_all(sib_2)
    left_both(group2)
    first_of(group2)
    correlate(group0)
    second_of(group0)
    acc1 = ring_second(1, 0, 1, zl, hop1)
    acc3 = ring_second(3, 2, 3, zl, hop3)
    correlate(group1)
    correlate(group2)

    def pairs():
        for m in range(2):

            def step(p, acc, m=m):
                return acc + fold(lg[p, 2 * c + m].astype(F32) * r[m, p].astype(F32))

            sums[1] += lax.fori_loop(0, 16, step, jnp.zeros((8, 128), F32))

    pl.when(blk // 2 == grp)(pairs)
    sum_copy = send(sums.at[pl.ds(0, 2)], sums.at[pl.ds(2, 2)], sibling)

    second_of(group1)

    sum_copy.wait_recv()
    sums[4:6] = sums[0:2] + sums[2:4]
    sum_copy = send(sums.at[pl.ds(4, 2)], sums.at[pl.ds(6, 2)], z_dev)

    ring_third(0, 0, 1, zo, dir0, acc0)
    z_got0 = z_send(0, 0, 1)
    ring_third(2, 2, 3, zo, dir2, acc2)
    z_got1 = z_send(1, 2, 3)

    second_of(group2)

    sum_copy.wait_recv()
    sums[8:10] = sums[4:6] + sums[6:8]
    sum_copy = send(sums.at[pl.ds(8, 2)], sums.at[pl.ds(10, 2)], h_dev)

    own = (y + 4 - x) % 4

    def y_total(z):
        def step(k, carry):
            m, core = k // 2, k % 2
            at = sl.at[own, z, m, core]
            decode_add(at, at, [(yr.at[i, z, m, core], ysr.at[i, z, m, core]) for i in range(2)])
            return carry

        lax.fori_loop(0, 4, step, 0)

    def y_arrived(z):
        for side in range(2):
            for m in range(2):
                for copy in to_owner(0, z, m, side, y_devs[0]):
                    copy.wait_recv()

    y_arrived(1 - zh)
    y_total(1 - zh)

    def h_encode(k, carry):
        m, core = k // 2, k % 2
        encode(sl.at[own, 1 - zh, m, core], hs.at[m, core], hss.at[m, core])
        return carry

    lax.fori_loop(0, 4, h_encode, 0)
    h_got = [send(hs, hr, h_dev), send(hss, hsr, h_dev)]

    sum_copy.wait_recv()
    xs[x] = sums[8:10] + sums[10:12]
    x_sums = [send(xs.at[x], xs.at[x], device) for device in (xp_dev, xm_dev, x2_dev)]

    ring_third(1, 0, 1, zl, dir1, acc1)
    ring_third(3, 2, 3, zl, dir3, acc3)

    await_all(x_sums)
    ysum[y] = xs[0] + xs[1] + xs[2] + xs[3]
    y_sums = [send(ysum.at[y], ysum.at[y], device) for device in y_devs]

    z_take(0, 0, 1, z_got0)
    z_take(1, 2, 3, z_got1)
    sr_copies = []
    for j in range(4):
        copy = pltpu.make_async_copy(tot.at[j, xz(0, zl)], sr_out.at[j], load_sem.at[j])
        copy.start()
        sr_copies.append(copy)

    y_arrived(zh)
    y_total(zh)

    await_all(y_sums)
    both = ysum[0] + ysum[1] + ysum[2] + ysum[3]
    numerator = jnp.sum(jnp.sum(both[0], axis=0, keepdims=True), axis=1, keepdims=True)
    denominator = jnp.sum(jnp.sum(both[1], axis=0, keepdims=True), axis=1, keepdims=True)
    ray[0] = (numerator / denominator)[0, 0]
    ray_copy = pltpu.make_async_copy(ray, ray_out, load_sem.at[8])
    ray_copy.start()

    await_all(h_got)
    sl_copies = []
    for m in range(2):
        keep = screen_ref[0, 2 * blk + m].astype(F32)
        for core in range(2):
            at = sl.at[own, zh, m, core]
            decode_add(at, at, [(hr.at[m, core], hsr.at[m, core])], keep)
            copy = pltpu.make_async_copy(at, sl_out.at[m, core], load_sem.at[4 + m * 2 + core])
            copy.start()
            sl_copies.append(copy)
    for copy in sr_copies + sl_copies + [ray_copy]:
        copy.wait()

    def drain():
        for copy in started:
            copy.wait_send()
        for j in range(4):
            part_copy(j).wait_send()
        for dx, z in group0 + group1 + group2:
            y_drain(dx, z)

    drain()


def body(right_vector, left_vector, cycle_weights, screen):
    right = right_vector.reshape(768, 2, 768)
    left = left_vector.reshape(48, 4, 768)
    anywhere = pl.BlockSpec(memory_space=pl.ANY)
    scratch = [
        pltpu.VMEM((2, 4, 768, 768), BF16),
        pltpu.VMEM((768, 2, 768), BF16),
        pltpu.VMEM((48, 4, 768), BF16),
        pltpu.VMEM((2, 16, 48, 768), BF16),
        pltpu.VMEM((2, 16, 48, 768), BF16),
        pltpu.VMEM((16, 4, 48, 768), BF16),
        pltpu.VMEM((4, 8, 2, 48, 768), F32),
        pltpu.VMEM((4, 8, 48, 768), F32),
        pltpu.VMEM((4, 2, 2, 2, 48, 768), F32),
        pltpu.VMEM((4, 6, 48, 768), I16),
        pltpu.VMEM((4, 6, 48, 768), I16),
        pltpu.VMEM((4, 6, 8, 128), F32),
        pltpu.VMEM((4, 6, 8, 128), F32),
        pltpu.VMEM((2, 2, 48, 768), I16),
        pltpu.VMEM((2, 2, 48, 768), I16),
        pltpu.VMEM((2, 2, 8, 128), F32),
        pltpu.VMEM((2, 2, 8, 128), F32),
        pltpu.VMEM((4, 2, 2, 2, 48, 768), I16),
        pltpu.VMEM((2, 2, 2, 2, 48, 768), I16),
        pltpu.VMEM((2, 2, 2, 48, 768), I16),
        pltpu.VMEM((4, 2, 2, 2, 8, 128), F32),
        pltpu.VMEM((2, 2, 2, 2, 8, 128), F32),
        pltpu.VMEM((2, 2, 2, 8, 128), F32),
        pltpu.VMEM((2, 2, 48, 768), I16),
        pltpu.VMEM((2, 2, 48, 768), I16),
        pltpu.VMEM((2, 2, 8, 128), F32),
        pltpu.VMEM((2, 2, 8, 128), F32),
        pltpu.VMEM((12, 8, 128), F32),
        pltpu.VMEM((4, 2, 8, 128), F32),
        pltpu.VMEM((4, 2, 8, 128), F32),
        pltpu.SMEM((1,), F32),
        pltpu.SemaphoreType.DMA((10,)),
        pltpu.SemaphoreType.DMA((N_SEM,)),
        pltpu.SemaphoreType.DMA((N_SEM,)),
        pltpu.SemaphoreType.DMA((4, 2, 2, 2)),
        pltpu.SemaphoreType.DMA((2, 2, 2, 2)),
        pltpu.SemaphoreType.DMA((2, 2, 2)),
        pltpu.SemaphoreType.DMA((4, 2)),
    ]
    sr, sl, ray = pl.pallas_call(
        kernel,
        out_shape=(
            jax.ShapeDtypeStruct((4, 48, 768), F32),
            jax.ShapeDtypeStruct((2, 2, 48, 768), F32),
            jax.ShapeDtypeStruct((1,), F32),
        ),
        in_specs=[pl.BlockSpec(memory_space=pltpu.SMEM), anywhere, anywhere, anywhere],
        out_specs=(anywhere, anywhere, anywhere),
        scratch_shapes=scratch,
        compiler_params=pltpu.CompilerParams(
            collective_id=0, has_side_effects=True, vmem_limit_bytes=60 * 2**20
        ),
        cost_estimate=pl.CostEstimate(
            flops=14_500_000_000, bytes_accessed=13_000_000, transcendentals=0
        ),
    )(screen, right, left, cycle_weights)
    sigma_right = sr.transpose(1, 0, 2)[:, None]
    sigma_left = sl.reshape(2, 96, 768).transpose(1, 0, 2)[:, None]
    return sigma_right, sigma_left, ray


def solution(mesh):
    in_specs = (
        P(None, None, "blk", None),
        P("blk", None, "grp", None),
        P("blk", "grp", None, None),
        P(),
    )
    out_specs = (P("blk", None, "grp", None), P("grp", None, "blk", None), P())
    return jax.shard_map(body, mesh=mesh, in_specs=in_specs, out_specs=out_specs, check_vma=False)
```

```python
import functools

import jax
import jax.numpy as jnp
from jax import lax
from jax.experimental import pallas as pl
from jax.experimental.pallas import tpu as pltpu
from jax.sharding import PartitionSpec as P

MESH = pl.DeviceIdType.MESH
F32 = jnp.float32
BF16 = jnp.bfloat16
I16 = jnp.int16
LEVELS = 32000.0
N_SEM = 94


def dot_nn(a, b):
    return jnp.dot(a, b, preferred_element_type=F32)


def dot_nt(a, b):
    return lax.dot_general(a, b, (((1,), (1,)), ((), ())), preferred_element_type=F32)


def wide(scale):
    return jnp.concatenate([scale] * 6, axis=1)


def band(i):
    return pl.ds(pl.multiple_of(i * 16, 16), 16)


def encode(src, q_ref, scale_ref):
    def top_step(i, top):
        return jnp.maximum(top, jnp.abs(src[band(i)]))

    top = lax.fori_loop(0, 3, top_step, jnp.full((16, 768), 1e-30, F32))
    top = jnp.max(top, axis=0, keepdims=True)
    top = functools.reduce(jnp.maximum, [top[:, i * 128 : (i + 1) * 128] for i in range(6)])
    inverse = wide(LEVELS / top)
    scale_ref[...] = jnp.broadcast_to(top * (1.0 / LEVELS), (8, 128))

    def step(i, carry):
        q_ref[band(i)] = jnp.round(src[band(i)] * inverse).astype(jnp.int32).astype(I16)
        return carry

    lax.fori_loop(0, 3, step, 0)


def decode_add(dst, src, terms, factor=1.0):
    scales = [wide(scale[0:1]) for _, scale in terms]

    def step(i, carry):
        total = src[band(i)]
        for (q, _), scale in zip(terms, scales):
            total = total + q[band(i)].astype(jnp.int32).astype(F32) * scale
        dst[band(i)] = total * factor
        return carry

    lax.fori_loop(0, 3, step, 0)


def fold(x):
    rows = functools.reduce(jnp.add, [x[i * 8 : (i + 1) * 8] for i in range(6)])
    return functools.reduce(jnp.add, [rows[:, i * 128 : (i + 1) * 128] for i in range(6)])


def kernel(
    screen_ref, right_hbm, left_hbm, weights_hbm, sr_out, sl_out, ray_out,
    w, right_raw, left_raw, r, rs, lg, part, tot, sl,
    ring_s, ring_r, rsc_s, rsc_r,
    zf_s, zf_r, zfs_s, zfs_r,
    ys, yr, yh, yss, ysr, yhs,
    hs, hr, hss, hsr,
    sums, xs, ysum, ray,
    load_sem, send_sem, recv_sem, ysend_sem, yrecv_sem, yhop_sem, part_sem,
):
    blk = lax.axis_index("blk")
    grp = lax.axis_index("grp")
    x, zl, c = blk // 4, (blk // 2) % 2, blk % 2
    y, zh = grp // 2, grp % 2
    zo = 1 - zl
    sibling = (blk + 1 - 2 * c, grp)
    z_dev = (blk + 2 - 4 * zl, grp)
    xp_dev = ((blk + 4) % 16, grp)
    xm_dev = ((blk + 12) % 16, grp)
    x2_dev = ((blk + 8) % 16, grp)
    y_devs = [(blk, (grp + 2 * k) % 8) for k in (1, 2, 3)]
    h_dev = (blk, grp + 1 - 2 * zh)

    loads = []

    def load(src, dst):
        copy = pltpu.make_async_copy(src, dst, load_sem.at[len(loads)])
        copy.start()
        loads.append(copy)
        return copy

    def pos(dx, z, core):
        return ((x + dx) % 4) * 4 + z * 2 + core

    here = pos(0, zl, c)
    left_in = load(left_hbm, left_raw)
    right_in = load(right_hbm, right_raw)

    def weight_copy(j, m):
        return pltpu.make_async_copy(weights_hbm.at[m, j], w.at[m, j], load_sem.at[2 + j * 2 + m])

    for j in range(4):
        for m in range(2):
            weight_copy(j, m).start()

    barrier = pltpu.get_barrier_semaphore()
    partners = [sibling, z_dev, xp_dev, xm_dev, x2_dev, h_dev] + y_devs
    for partner in partners:
        pl.semaphore_signal(barrier, inc=1, device_id=partner, device_id_type=MESH)
    left_in.wait()
    for j in range(4):
        lg[here, j] = left_raw[:, j, :]
    pl.semaphore_wait(barrier, len(partners))

    started = []

    def send(src, dst, device):
        k = len(started)
        copy = pltpu.make_async_remote_copy(
            src_ref=src, dst_ref=dst, send_sem=send_sem.at[k], recv_sem=recv_sem.at[k],
            device_id=device, device_id_type=MESH,
        )
        copy.start()
        started.append(copy)
        return copy

    def hand(p, device, j=0, count=4):
        ref = lg.at[p, pl.ds(j, count)]
        return send(ref, ref, device)

    def await_all(copies):
        for copy in copies:
            copy.wait_recv()

    own_xp = [hand(here, xp_dev, 0, 2), hand(here, xp_dev, 2, 2)]
    own_xm = [hand(here, xm_dev, 2, 2), hand(here, xm_dev, 0, 2)]
    own_z = [hand(here, z_dev, 0, 2), hand(here, z_dev, 2, 2)]
    sib_0 = [hand(here, sibling)]
    sib_1 = []

    def part_copy(j):
        return pltpu.make_async_remote_copy(
            src_ref=part.at[j, :, 1 - c], dst_ref=tot.at[j], send_sem=part_sem.at[j, 0],
            recv_sem=part_sem.at[j, 1], device_id=sibling, device_id_type=MESH,
        )

    def right_parts(first, last):
        def step(j, carry):
            acc = dot_nn(rs[0].reshape(768, 768), w[0, j]) + dot_nn(rs[1].reshape(768, 768), w[1, j])
            part[j] = acc.reshape(8, 2, 48, 768)
            part_copy(j).start()
            return carry

        lax.fori_loop(first, last, step, 0)

    def join_parts(first):
        for j in range(first, first + 2):
            part_copy(j).wait_recv()

        def step(k, carry):
            j, at = first + k // 8, k % 8
            tot[j, at] = tot[j, at] + part[j, at, c]
            return carry

        lax.fori_loop(0, 16, step, 0)

    sums[0:2] = jnp.zeros((2, 8, 128), F32)

    def left_rows(chunks, m):
        rows = [pos(dx, z, core) for dx, z in chunks for core in range(2)]
        acc = None
        for j in range(4):
            block = jnp.concatenate([lg[p, j] for p in rows], axis=0)
            term = dot_nt(block, w[m, j])
            acc = term if acc is None else acc + term
        for i in range(len(rows)):
            dx, z = chunks[i // 2]
            sl[dx % 4, z, m, i % 2] = acc[i * 48 : (i + 1) * 48]

    def left_both(chunks):
        def step(m, carry):
            left_rows(chunks, m)
            return carry

        lax.fori_loop(0, 2, step, 0)

    def correlate(chunks):
        for dx, z in chunks:

            def step(k, acc, dx=dx, z=z):
                m, core = k // 2, k % 2
                return acc + fold(sl[dx % 4, z, m, core] * rs[m, pos(dx, z, core)].astype(F32))

            sums[0] += lax.fori_loop(0, 4, step, jnp.zeros((8, 128), F32))

    def role(dx):
        owner = (x + dx) % 4
        step = (y + 4 - owner) % 4
        return owner, step, step // 2

    def y_copies(dx, z, m, core, dst, dst_scale, sems, device):
        at = (dx % 4, z, m, core)
        return [
            pltpu.make_async_remote_copy(
                src_ref=src.at[at], dst_ref=to, send_sem=ysend_sem.at[at + (i,)], recv_sem=sems.at[i],
                device_id=device, device_id_type=MESH,
            )
            for i, (src, to) in enumerate(((ys, dst), (yss, dst_scale)))
        ]

    def to_owner(dx, z, m, core, side, device):
        at = (side, z, m, core)
        return y_copies(dx, z, m, core, yr.at[at], ysr.at[at], yrecv_sem.at[at], device)

    def to_side(dx, z, m, core, device):
        at = (z, m, core)
        return y_copies(dx, z, m, core, yh.at[at], yhs.at[at], yhop_sem.at[at], device)

    def y_encode(d, z, m, core):
        encode(sl.at[d, z, m, core], ys.at[d, z, m, core], yss.at[d, z, m, core])

    def y_far(dx, z):
        owner, step, side = role(dx)

        def far():
            for m in range(2):

                def piece(core, carry, m=m):
                    y_encode(dx % 4, z, m, core)
                    for copy in to_side(dx, z, m, core, y_devs[2 * m]):
                        copy.start()
                    return carry

                lax.fori_loop(0, 2, piece, 0)

        pl.when(step == 2)(far)

    def y_near(dx, z):
        owner, step, side = role(dx)

        def near():
            def piece(core, carry):
                y_encode(dx % 4, z, side, core)
                for copy in to_owner(dx, z, side, core, side, (blk, owner * 2 + zh)):
                    copy.start()
                return carry

            lax.fori_loop(0, 2, piece, 0)

        pl.when(step % 2 == 1)(near)

    def y_second(dx, z, core):
        owner, step, side = role(dx)
        d = dx % 4
        other = 1 - side

        def near():
            for copy in to_side(dx, z, other, core, y_devs[0]):
                copy.wait_recv()
            at = sl.at[d, z, other, core]
            decode_add(at, at, [(yh.at[z, other, core], yhs.at[z, other, core])])
            y_encode(d, z, other, core)
            for copy in to_owner(dx, z, other, core, side, (blk, owner * 2 + zh)):
                copy.start()

        pl.when(step % 2 == 1)(near)

    def y_drain(dx, z):
        owner, step, side = role(dx)

        def done():
            def piece(k, carry):
                for copy in to_side(dx, z, k // 2, k % 2, y_devs[0]):
                    copy.wait_send()
                return carry

            lax.fori_loop(0, 4, piece, 0)

        pl.when(step != 0)(done)

    def first_of(chunks):
        for dx, z in chunks:
            y_far(dx, z)
        for dx, z in chunks:
            y_near(dx, z)

    def second_of(chunks):
        for core in range(2):
            for dx, z in chunks:
                y_second(dx, z, core)

    def ring_send(n, kind, block, device):
        encode(block, ring_s.at[n, kind], rsc_s.at[n, kind])
        return [
            send(ring_s.at[n, kind], ring_r.at[n, kind], device),
            send(rsc_s.at[n, kind], rsc_r.at[n, kind], device),
        ]

    def ring_add(n, at, kinds):
        for _, copies in kinds:
            await_all(copies)
        decode_add(at, at, [(ring_r.at[n, kind], rsc_r.at[n, kind]) for kind, _ in kinds])

    def xz(dx, z):
        return ((x + dx) % 4) * 2 + z

    def ring_hop(n, ja, jb, z):
        hop_p = ring_send(n, 0, tot.at[ja, xz(2, z)], xp_dev)
        hop_m = ring_send(n, 1, tot.at[jb, xz(2, z)], xm_dev)
        return hop_p, hop_m

    def ring_direct(n, ja, jb, z):
        dir_p = ring_send(n, 2, tot.at[jb, xz(1, z)], xp_dev)
        dir_m = ring_send(n, 3, tot.at[ja, xz(-1, z)], xm_dev)
        return dir_p, dir_m

    def ring_second(n, ja, jb, z, hop):
        to_p, to_m = tot.at[ja, xz(1, z)], tot.at[jb, xz(-1, z)]
        ring_add(n, to_p, [(0, hop[0])])
        acc_p = ring_send(n, 4, to_p, xp_dev)
        ring_add(n, to_m, [(1, hop[1])])
        acc_m = ring_send(n, 5, to_m, xm_dev)
        return acc_p, acc_m

    def ring_third(n, ja, jb, z, direct, second):
        at = xz(0, z)
        ring_add(n, tot.at[ja, at], [(3, direct[1]), (4, second[0])])
        ring_add(n, tot.at[jb, at], [(2, direct[0]), (5, second[1])])

    def z_send(n, ja, jb):
        for i, j in enumerate((ja, jb)):
            encode(tot.at[j, xz(0, zo)], zf_s.at[n, i], zfs_s.at[n, i])
        return [send(zf_s.at[n], zf_r.at[n], z_dev), send(zfs_s.at[n], zfs_r.at[n], z_dev)]

    def z_take(n, ja, jb, copies):
        await_all(copies)
        for i, j in enumerate((ja, jb)):
            at = tot.at[j, xz(0, zl)]
            decode_add(at, at, [(zf_r.at[n, i], zfs_r.at[n, i])])

    right_in.wait()
    for m in range(2):

        def right_rows(k, carry, m=m):
            r[m, k] = right_raw[pl.ds(pl.multiple_of(k * 48, 48), 48), m, :]
            return carry

        lax.fori_loop(0, 16, right_rows, 0)

    own_z[0].wait_recv()
    z_xp = hand(pos(0, zo, c), xp_dev, 0, 2)
    own_xp[0].wait_recv()
    far_xp = hand(pos(-1, zl, c), xp_dev, 0, 2)
    own_xm[0].wait_recv()
    far_xm = hand(pos(1, zl, c), xm_dev, 2, 2)
    z_xm1 = hand(pos(0, zo, c), xm_dev, 1, 1)
    z_xm0 = hand(pos(0, zo, c), xm_dev, 0, 1)
    x_z1 = hand(pos(1, zl, c), z_dev, 2, 2)
    sib_1 += [hand(pos(0, zo, c), sibling, 0, 2), hand(pos(-1, zl, c), sibling, 0, 2)]
    sib_1 += [hand(pos(1, zl, c), sibling, 2, 2)]

    for m in range(2):
        keep = screen_ref[0, 2 * blk + m].astype(F32).astype(BF16)

        def screen_rows(k, carry, m=m, keep=keep):
            rs[m, k] = r[m, k] * keep
            return carry

        lax.fori_loop(0, 16, screen_rows, 0)
    for j in (0, 1):
        for m in range(2):
            weight_copy(j, m).wait()
    right_parts(0, 2)

    own_xp[1].wait_recv()
    x_z2 = hand(pos(-1, zl, c), z_dev, 2, 2)
    own_xm[1].wait_recv()
    own_z[1].wait_recv()
    sib_1 += [hand(pos(0, zo, c), sibling, 2, 2), hand(pos(-1, zl, c), sibling, 2, 2)]
    sib_1 += [hand(pos(1, zl, c), sibling, 0, 2)]

    for j in (2, 3):
        for m in range(2):
            weight_copy(j, m).wait()
    right_parts(2, 4)
    join_parts(0)

    far_xm.wait_recv()
    x_z3 = hand(pos(2, zl, c), z_dev, 2, 2)
    z_xp.wait_recv()
    zfar_xp = hand(pos(-1, zo, c), xp_dev, 0, 1)
    z_xm1.wait_recv()
    zfar_xm = hand(pos(1, zo, c), xm_dev, 1, 1)
    x_z1.wait_recv()
    sib_2 = [hand(pos(-1, zo, c), sibling, 0, 2), hand(pos(1, zo, c), sibling, 2, 2)]
    hop0 = ring_hop(0, 0, 1, zo)
    dir0 = ring_direct(0, 0, 1, zo)

    group0 = [(0, 1 - zh), (0, zh)]
    await_all(sib_0)
    await_all(sib_1)
    left_both(group0)

    far_xp.wait_recv()
    sib_far = hand(pos(2, zl, c), sibling)
    z_xm0.wait_recv()
    x_z2.wait_recv()
    sib_2 += [hand(pos(1, zo, c), sibling, 0, 2), hand(pos(-1, zo, c), sibling, 2, 2)]

    first_of(group0)
    join_parts(2)
    hop2 = ring_hop(2, 2, 3, zo)
    dir2 = ring_direct(2, 2, 3, zo)
    hop1 = ring_hop(1, 0, 1, zl)
    hop3 = ring_hop(3, 2, 3, zl)

    zfar_xp.wait_recv()
    zfar_xm.wait_recv()
    x_z3.wait_recv()
    sib_2.append(hand(pos(2, zo, c), sibling))

    group1 = [(1, zl), (-1, zl), (2, zl)]
    sib_far.wait_recv()
    left_both(group1)
    first_of(group1)
    acc0 = ring_second(0, 0, 1, zo, hop0)
    acc2 = ring_second(2, 2, 3, zo, hop2)
    dir1 = ring_direct(1, 0, 1, zl)
    dir3 = ring_direct(3, 2, 3, zl)

    group2 = [(2, zo), (1, zo), (-1, zo)]
    await_all(sib_2)
    left_both(group2)
    first_of(group2)
    correlate(group0)
    second_of(group0)
    acc1 = ring_second(1, 0, 1, zl, hop1)
    acc3 = ring_second(3, 2, 3, zl, hop3)
    correlate(group1)
    correlate(group2)

    def pairs():
        for m in range(2):

            def step(p, acc, m=m):
                return acc + fold(lg[p, 2 * c + m].astype(F32) * r[m, p].astype(F32))

            sums[1] += lax.fori_loop(0, 16, step, jnp.zeros((8, 128), F32))

    pl.when(blk // 2 == grp)(pairs)
    sum_copy = send(sums.at[pl.ds(0, 2)], sums.at[pl.ds(2, 2)], sibling)

    second_of(group1)

    sum_copy.wait_recv()
    sums[4:6] = sums[0:2] + sums[2:4]
    sum_copy = send(sums.at[pl.ds(4, 2)], sums.at[pl.ds(6, 2)], z_dev)

    ring_third(0, 0, 1, zo, dir0, acc0)
    z_got0 = z_send(0, 0, 1)
    ring_third(2, 2, 3, zo, dir2, acc2)
    z_got1 = z_send(1, 2, 3)

    second_of(group2)

    sum_copy.wait_recv()
    sums[8:10] = sums[4:6] + sums[6:8]
    sum_copy = send(sums.at[pl.ds(8, 2)], sums.at[pl.ds(10, 2)], h_dev)

    own = (y + 4 - x) % 4

    def y_total(z, core):
        for side in range(2):
            for m in range(2):
                for copy in to_owner(0, z, m, core, side, y_devs[0]):
                    copy.wait_recv()

        def step(m, carry):
            at = sl.at[own, z, m, core]
            decode_add(at, at, [(yr.at[i, z, m, core], ysr.at[i, z, m, core]) for i in range(2)])
            return carry

        lax.fori_loop(0, 2, step, 0)

    h_got = []
    for core in range(2):
        y_total(1 - zh, core)

        def h_encode(m, carry, core=core):
            encode(sl.at[own, 1 - zh, m, core], hs.at[core, m], hss.at[core, m])
            return carry

        lax.fori_loop(0, 2, h_encode, 0)
        h_got.append(
            [send(hs.at[core], hr.at[core], h_dev), send(hss.at[core], hsr.at[core], h_dev)]
        )

    sum_copy.wait_recv()
    xs[x] = sums[8:10] + sums[10:12]
    x_sums = [send(xs.at[x], xs.at[x], device) for device in (xp_dev, xm_dev, x2_dev)]

    ring_third(1, 0, 1, zl, dir1, acc1)
    ring_third(3, 2, 3, zl, dir3, acc3)

    await_all(x_sums)
    ysum[y] = xs[0] + xs[1] + xs[2] + xs[3]
    y_sums = [send(ysum.at[y], ysum.at[y], device) for device in y_devs]

    z_take(0, 0, 1, z_got0)
    z_take(1, 2, 3, z_got1)
    sr_copies = []
    for j in range(4):
        copy = pltpu.make_async_copy(tot.at[j, xz(0, zl)], sr_out.at[:, j], load_sem.at[j])
        copy.start()
        sr_copies.append(copy)

    for core in range(2):
        y_total(zh, core)

    await_all(y_sums)
    both = ysum[0] + ysum[1] + ysum[2] + ysum[3]
    numerator = jnp.sum(jnp.sum(both[0], axis=0, keepdims=True), axis=1, keepdims=True)
    denominator = jnp.sum(jnp.sum(both[1], axis=0, keepdims=True), axis=1, keepdims=True)
    ray[0] = (numerator / denominator)[0, 0]
    ray_copy = pltpu.make_async_copy(ray, ray_out, load_sem.at[8])
    ray_copy.start()

    sl_copies = []
    for core in range(2):
        await_all(h_got[core])
        for m in range(2):
            keep = screen_ref[0, 2 * blk + m].astype(F32)
            at = sl.at[own, zh, m, core]
            decode_add(at, at, [(hr.at[core, m], hsr.at[core, m])], keep)
            copy = pltpu.make_async_copy(
                at, sl_out.at[pl.ds(core * 48, 48), m], load_sem.at[4 + m * 2 + core]
            )
            copy.start()
            sl_copies.append(copy)
    for copy in sr_copies + sl_copies + [ray_copy]:
        copy.wait()

    def drain():
        for copy in started:
            copy.wait_send()
        for j in range(4):
            part_copy(j).wait_send()
        for dx, z in group0 + group1 + group2:
            y_drain(dx, z)

    drain()


def hand_out(sr_ref, sl_ref, sr_out, sl_out, sr_block, sl_block, sems):
    into = [
        pltpu.make_async_copy(sr_ref, sr_block, sems.at[0]),
        pltpu.make_async_copy(sl_ref, sl_block, sems.at[1]),
    ]
    out = [
        pltpu.make_async_copy(sr_block, sr_out, sems.at[2]),
        pltpu.make_async_copy(sl_block, sl_out, sems.at[3]),
    ]
    for copy in into:
        copy.start()
    for first, second in zip(into, out):
        first.wait()
        second.start()
    for copy in out:
        copy.wait()


def body(right_vector, left_vector, cycle_weights, screen):
    right = right_vector.reshape(768, 2, 768)
    left = left_vector.reshape(48, 4, 768)
    anywhere = pl.BlockSpec(memory_space=pl.ANY)
    scratch = [
        pltpu.VMEM((2, 4, 768, 768), BF16),
        pltpu.VMEM((768, 2, 768), BF16),
        pltpu.VMEM((48, 4, 768), BF16),
        pltpu.VMEM((2, 16, 48, 768), BF16),
        pltpu.VMEM((2, 16, 48, 768), BF16),
        pltpu.VMEM((16, 4, 48, 768), BF16),
        pltpu.VMEM((4, 8, 2, 48, 768), F32),
        pltpu.VMEM((4, 8, 48, 768), F32),
        pltpu.VMEM((4, 2, 2, 2, 48, 768), F32),
        pltpu.VMEM((4, 6, 48, 768), I16),
        pltpu.VMEM((4, 6, 48, 768), I16),
        pltpu.VMEM((4, 6, 8, 128), F32),
        pltpu.VMEM((4, 6, 8, 128), F32),
        pltpu.VMEM((2, 2, 48, 768), I16),
        pltpu.VMEM((2, 2, 48, 768), I16),
        pltpu.VMEM((2, 2, 8, 128), F32),
        pltpu.VMEM((2, 2, 8, 128), F32),
        pltpu.VMEM((4, 2, 2, 2, 48, 768), I16),
        pltpu.VMEM((2, 2, 2, 2, 48, 768), I16),
        pltpu.VMEM((2, 2, 2, 48, 768), I16),
        pltpu.VMEM((4, 2, 2, 2, 8, 128), F32),
        pltpu.VMEM((2, 2, 2, 2, 8, 128), F32),
        pltpu.VMEM((2, 2, 2, 8, 128), F32),
        pltpu.VMEM((2, 2, 48, 768), I16),
        pltpu.VMEM((2, 2, 48, 768), I16),
        pltpu.VMEM((2, 2, 8, 128), F32),
        pltpu.VMEM((2, 2, 8, 128), F32),
        pltpu.VMEM((12, 8, 128), F32),
        pltpu.VMEM((4, 2, 8, 128), F32),
        pltpu.VMEM((4, 2, 8, 128), F32),
        pltpu.SMEM((1,), F32),
        pltpu.SemaphoreType.DMA((10,)),
        pltpu.SemaphoreType.DMA((N_SEM,)),
        pltpu.SemaphoreType.DMA((N_SEM,)),
        pltpu.SemaphoreType.DMA((4, 2, 2, 2, 2)),
        pltpu.SemaphoreType.DMA((2, 2, 2, 2, 2)),
        pltpu.SemaphoreType.DMA((2, 2, 2, 2)),
        pltpu.SemaphoreType.DMA((4, 2)),
    ]
    sr, sl, ray = pl.pallas_call(
        kernel,
        out_shape=(
            jax.ShapeDtypeStruct((48, 4, 768), F32),
            jax.ShapeDtypeStruct((96, 2, 768), F32),
            jax.ShapeDtypeStruct((1,), F32),
        ),
        in_specs=[pl.BlockSpec(memory_space=pltpu.SMEM), anywhere, anywhere, anywhere],
        out_specs=(anywhere, anywhere, anywhere),
        scratch_shapes=scratch,
        compiler_params=pltpu.CompilerParams(
            collective_id=0, has_side_effects=True, vmem_limit_bytes=60 * 2**20
        ),
        cost_estimate=pl.CostEstimate(
            flops=14_500_000_000, bytes_accessed=13_000_000, transcendentals=0
        ),
    )(screen, right, left, cycle_weights)
    sigma_right, sigma_left = pl.pallas_call(
        hand_out,
        out_shape=(jax.ShapeDtypeStruct(sr.shape, F32), jax.ShapeDtypeStruct(sl.shape, F32)),
        in_specs=[anywhere, anywhere],
        out_specs=(anywhere, anywhere),
        scratch_shapes=[
            pltpu.VMEM(sr.shape, F32),
            pltpu.VMEM(sl.shape, F32),
            pltpu.SemaphoreType.DMA((4,)),
        ],
    )(sr, sl)
    return sigma_right[:, None], sigma_left[:, None], ray


def solution(mesh):
    in_specs = (
        P(None, None, "blk", None),
        P("blk", None, "grp", None),
        P("blk", "grp", None, None),
        P(),
    )
    out_specs = (P("blk", None, "grp", None), P("grp", None, "blk", None), P())
    return jax.shard_map(body, mesh=mesh, in_specs=in_specs, out_specs=out_specs, check_vma=False)
```

```python
import functools

import jax
import jax.numpy as jnp
from jax import lax
from jax.experimental import pallas as pl
from jax.experimental.pallas import tpu as pltpu
from jax.sharding import PartitionSpec as P

MESH = pl.DeviceIdType.MESH
F32 = jnp.float32
BF16 = jnp.bfloat16
I16 = jnp.int16
LEVELS = 32000.0
N_SEM = 94


def dot_nn(a, b):
    return jnp.dot(a, b, preferred_element_type=F32)


def dot_nt(a, b):
    return lax.dot_general(a, b, (((1,), (1,)), ((), ())), preferred_element_type=F32)


def wide(scale):
    return jnp.concatenate([scale] * 6, axis=1)


def band(i):
    return pl.ds(pl.multiple_of(i * 16, 16), 16)


def encode(src, q_ref, scale_ref):
    def top_step(i, top):
        return jnp.maximum(top, jnp.abs(src[band(i)]))

    top = lax.fori_loop(0, 3, top_step, jnp.full((16, 768), 1e-30, F32))
    top = jnp.max(top, axis=0, keepdims=True)
    top = functools.reduce(jnp.maximum, [top[:, i * 128 : (i + 1) * 128] for i in range(6)])
    inverse = wide(LEVELS / top)
    scale_ref[...] = jnp.broadcast_to(top * (1.0 / LEVELS), (8, 128))

    def step(i, carry):
        q_ref[band(i)] = jnp.round(src[band(i)] * inverse).astype(jnp.int32).astype(I16)
        return carry

    lax.fori_loop(0, 3, step, 0)


def decode_add(dst, src, terms, factor=1.0):
    scales = [wide(scale[0:1]) for _, scale in terms]

    def step(i, carry):
        total = src[band(i)]
        for (q, _), scale in zip(terms, scales):
            total = total + q[band(i)].astype(jnp.int32).astype(F32) * scale
        dst[band(i)] = total * factor
        return carry

    lax.fori_loop(0, 3, step, 0)


def fold(x):
    rows = functools.reduce(jnp.add, [x[i * 8 : (i + 1) * 8] for i in range(6)])
    return functools.reduce(jnp.add, [rows[:, i * 128 : (i + 1) * 128] for i in range(6)])


def kernel(
    screen_ref, right_hbm, left_hbm, weights_hbm, sr_out, sl_out, ray_out,
    w, right_raw, left_raw, r, rs, lg, part, tot, sl,
    ring_s, ring_r, rsc_s, rsc_r,
    zf_s, zf_r, zfs_s, zfs_r,
    ys, yr, yh, yss, ysr, yhs,
    hs, hr, hss, hsr,
    sums, xs, ysum, ray,
    load_sem, send_sem, recv_sem, ysend_sem, yrecv_sem, yhop_sem, part_sem,
):
    blk = lax.axis_index("blk")
    grp = lax.axis_index("grp")
    x, zl, c = blk // 4, (blk // 2) % 2, blk % 2
    y, zh = grp // 2, grp % 2
    zo = 1 - zl
    sibling = (blk + 1 - 2 * c, grp)
    z_dev = (blk + 2 - 4 * zl, grp)
    xp_dev = ((blk + 4) % 16, grp)
    xm_dev = ((blk + 12) % 16, grp)
    x2_dev = ((blk + 8) % 16, grp)
    y_devs = [(blk, (grp + 2 * k) % 8) for k in (1, 2, 3)]
    h_dev = (blk, grp + 1 - 2 * zh)

    loads = []

    def load(src, dst):
        copy = pltpu.make_async_copy(src, dst, load_sem.at[len(loads)])
        copy.start()
        loads.append(copy)
        return copy

    def pos(dx, z, core):
        return ((x + dx) % 4) * 4 + z * 2 + core

    here = pos(0, zl, c)
    left_in = load(left_hbm, left_raw)
    right_in = load(right_hbm, right_raw)

    def weight_copy(j, m):
        return pltpu.make_async_copy(weights_hbm.at[m, j], w.at[m, j], load_sem.at[2 + j * 2 + m])

    for j in range(4):
        for m in range(2):
            weight_copy(j, m).start()

    barrier = pltpu.get_barrier_semaphore()
    partners = [sibling, z_dev, xp_dev, xm_dev, x2_dev, h_dev] + y_devs
    for partner in partners:
        pl.semaphore_signal(barrier, inc=1, device_id=partner, device_id_type=MESH)
    left_in.wait()
    for j in range(4):
        lg[here, j] = left_raw[:, j, :]
    pl.semaphore_wait(barrier, len(partners))

    started = []

    def send(src, dst, device):
        k = len(started)
        copy = pltpu.make_async_remote_copy(
            src_ref=src, dst_ref=dst, send_sem=send_sem.at[k], recv_sem=recv_sem.at[k],
            device_id=device, device_id_type=MESH,
        )
        copy.start()
        started.append(copy)
        return copy

    def hand(p, device, j=0, count=4):
        ref = lg.at[p, pl.ds(j, count)]
        return send(ref, ref, device)

    def await_all(copies):
        for copy in copies:
            copy.wait_recv()

    own_xp = [hand(here, xp_dev, 0, 2), hand(here, xp_dev, 2, 2)]
    own_xm = [hand(here, xm_dev, 2, 2), hand(here, xm_dev, 0, 2)]
    own_z = [hand(here, z_dev, 0, 2), hand(here, z_dev, 2, 2)]
    sib_0 = [hand(here, sibling)]
    sib_1 = []

    def part_copy(j):
        return pltpu.make_async_remote_copy(
            src_ref=part.at[j, :, 1 - c], dst_ref=tot.at[j], send_sem=part_sem.at[j, 0],
            recv_sem=part_sem.at[j, 1], device_id=sibling, device_id_type=MESH,
        )

    def right_parts(first, last):
        def step(j, carry):
            acc = dot_nn(rs[0].reshape(768, 768), w[0, j]) + dot_nn(rs[1].reshape(768, 768), w[1, j])
            part[j] = acc.reshape(8, 2, 48, 768)
            part_copy(j).start()
            return carry

        lax.fori_loop(first, last, step, 0)

    def join_parts(first):
        for j in range(first, first + 2):
            part_copy(j).wait_recv()

        def step(k, carry):
            j, at = first + k // 8, k % 8
            tot[j, at] = tot[j, at] + part[j, at, c]
            return carry

        lax.fori_loop(0, 16, step, 0)

    sums[0:2] = jnp.zeros((2, 8, 128), F32)

    def left_rows(chunks, m):
        rows = [pos(dx, z, core) for dx, z in chunks for core in range(2)]
        acc = None
        for j in range(4):
            block = jnp.concatenate([lg[p, j] for p in rows], axis=0)
            term = dot_nt(block, w[m, j])
            acc = term if acc is None else acc + term
        for i in range(len(rows)):
            dx, z = chunks[i // 2]
            sl[dx % 4, z, m, i % 2] = acc[i * 48 : (i + 1) * 48]

    def left_both(chunks):
        def step(m, carry):
            left_rows(chunks, m)
            return carry

        lax.fori_loop(0, 2, step, 0)

    def correlate(chunks):
        for dx, z in chunks:

            def step(k, acc, dx=dx, z=z):
                m, core = k // 2, k % 2
                return acc + fold(sl[dx % 4, z, m, core] * rs[m, pos(dx, z, core)].astype(F32))

            sums[0] += lax.fori_loop(0, 4, step, jnp.zeros((8, 128), F32))

    def role(dx):
        owner = (x + dx) % 4
        step = (y + 4 - owner) % 4
        return owner, step, step // 2

    def y_copies(dx, z, m, core, dst, dst_scale, sems, device):
        at = (dx % 4, z, m, core)
        return [
            pltpu.make_async_remote_copy(
                src_ref=src.at[at], dst_ref=to, send_sem=ysend_sem.at[at + (i,)], recv_sem=sems.at[i],
                device_id=device, device_id_type=MESH,
            )
            for i, (src, to) in enumerate(((ys, dst), (yss, dst_scale)))
        ]

    def to_owner(dx, z, m, core, side, device):
        at = (side, z, m, core)
        return y_copies(dx, z, m, core, yr.at[at], ysr.at[at], yrecv_sem.at[at], device)

    def to_side(dx, z, m, core, device):
        at = (z, m, core)
        return y_copies(dx, z, m, core, yh.at[at], yhs.at[at], yhop_sem.at[at], device)

    def y_encode(d, z, m, core):
        encode(sl.at[d, z, m, core], ys.at[d, z, m, core], yss.at[d, z, m, core])

    def y_far(dx, z):
        owner, step, side = role(dx)

        def far():
            for m in range(2):

                def piece(core, carry, m=m):
                    y_encode(dx % 4, z, m, core)
                    for copy in to_side(dx, z, m, core, y_devs[2 * m]):
                        copy.start()
                    return carry

                lax.fori_loop(0, 2, piece, 0)

        pl.when(step == 2)(far)

    def y_near(dx, z):
        owner, step, side = role(dx)

        def near():
            def piece(core, carry):
                y_encode(dx % 4, z, side, core)
                for copy in to_owner(dx, z, side, core, side, (blk, owner * 2 + zh)):
                    copy.start()
                return carry

            lax.fori_loop(0, 2, piece, 0)

        pl.when(step % 2 == 1)(near)

    def y_second(dx, z, core):
        owner, step, side = role(dx)
        d = dx % 4
        other = 1 - side

        def near():
            for copy in to_side(dx, z, other, core, y_devs[0]):
                copy.wait_recv()
            at = sl.at[d, z, other, core]
            decode_add(at, at, [(yh.at[z, other, core], yhs.at[z, other, core])])
            y_encode(d, z, other, core)
            for copy in to_owner(dx, z, other, core, side, (blk, owner * 2 + zh)):
                copy.start()

        pl.when(step % 2 == 1)(near)

    def y_drain(dx, z):
        owner, step, side = role(dx)

        def done():
            def piece(k, carry):
                for copy in to_side(dx, z, k // 2, k % 2, y_devs[0]):
                    copy.wait_send()
                return carry

            lax.fori_loop(0, 4, piece, 0)

        pl.when(step != 0)(done)

    def first_of(chunks):
        for dx, z in chunks:
            y_far(dx, z)
        for dx, z in chunks:
            y_near(dx, z)

    def second_of(chunks):
        for core in range(2):
            for dx, z in chunks:
                y_second(dx, z, core)

    def ring_send(n, kind, block, device):
        encode(block, ring_s.at[n, kind], rsc_s.at[n, kind])
        return [
            send(ring_s.at[n, kind], ring_r.at[n, kind], device),
            send(rsc_s.at[n, kind], rsc_r.at[n, kind], device),
        ]

    def ring_add(n, at, kinds):
        for _, copies in kinds:
            await_all(copies)
        decode_add(at, at, [(ring_r.at[n, kind], rsc_r.at[n, kind]) for kind, _ in kinds])

    def xz(dx, z):
        return ((x + dx) % 4) * 2 + z

    def ring_hop(n, ja, jb, z):
        hop_p = ring_send(n, 0, tot.at[ja, xz(2, z)], xp_dev)
        hop_m = ring_send(n, 1, tot.at[jb, xz(2, z)], xm_dev)
        return hop_p, hop_m

    def ring_direct(n, ja, jb, z):
        dir_p = ring_send(n, 2, tot.at[jb, xz(1, z)], xp_dev)
        dir_m = ring_send(n, 3, tot.at[ja, xz(-1, z)], xm_dev)
        return dir_p, dir_m

    def ring_second(n, ja, jb, z, hop):
        to_p, to_m = tot.at[ja, xz(1, z)], tot.at[jb, xz(-1, z)]
        ring_add(n, to_p, [(0, hop[0])])
        acc_p = ring_send(n, 4, to_p, xp_dev)
        ring_add(n, to_m, [(1, hop[1])])
        acc_m = ring_send(n, 5, to_m, xm_dev)
        return acc_p, acc_m

    def ring_third(n, ja, jb, z, direct, second):
        at = xz(0, z)
        ring_add(n, tot.at[ja, at], [(3, direct[1]), (4, second[0])])
        ring_add(n, tot.at[jb, at], [(2, direct[0]), (5, second[1])])

    def z_send(n, ja, jb):
        for i, j in enumerate((ja, jb)):
            encode(tot.at[j, xz(0, zo)], zf_s.at[n, i], zfs_s.at[n, i])
        return [send(zf_s.at[n], zf_r.at[n], z_dev), send(zfs_s.at[n], zfs_r.at[n], z_dev)]

    def z_take(n, ja, jb, copies):
        await_all(copies)
        for i, j in enumerate((ja, jb)):
            at = tot.at[j, xz(0, zl)]
            decode_add(at, at, [(zf_r.at[n, i], zfs_r.at[n, i])])

    right_in.wait()
    for m in range(2):

        def right_rows(k, carry, m=m):
            r[m, k] = right_raw[pl.ds(pl.multiple_of(k * 48, 48), 48), m, :]
            return carry

        lax.fori_loop(0, 16, right_rows, 0)

    own_z[0].wait_recv()
    z_xp = hand(pos(0, zo, c), xp_dev, 0, 2)
    own_xp[0].wait_recv()
    far_xp = hand(pos(-1, zl, c), xp_dev, 0, 2)
    own_xm[0].wait_recv()
    far_xm = hand(pos(1, zl, c), xm_dev, 2, 2)
    z_xm1 = hand(pos(0, zo, c), xm_dev, 1, 1)
    z_xm0 = hand(pos(0, zo, c), xm_dev, 0, 1)
    x_z1 = hand(pos(1, zl, c), z_dev, 2, 2)
    sib_1 += [hand(pos(0, zo, c), sibling, 0, 2), hand(pos(-1, zl, c), sibling, 0, 2)]
    sib_1 += [hand(pos(1, zl, c), sibling, 2, 2)]

    for m in range(2):
        keep = screen_ref[0, 2 * blk + m].astype(F32).astype(BF16)

        def screen_rows(k, carry, m=m, keep=keep):
            rs[m, k] = r[m, k] * keep
            return carry

        lax.fori_loop(0, 16, screen_rows, 0)
    for j in (0, 1):
        for m in range(2):
            weight_copy(j, m).wait()
    right_parts(0, 2)

    own_xp[1].wait_recv()
    x_z2 = hand(pos(-1, zl, c), z_dev, 2, 2)
    own_xm[1].wait_recv()
    own_z[1].wait_recv()
    sib_1 += [hand(pos(0, zo, c), sibling, 2, 2), hand(pos(-1, zl, c), sibling, 2, 2)]
    sib_1 += [hand(pos(1, zl, c), sibling, 0, 2)]

    for j in (2, 3):
        for m in range(2):
            weight_copy(j, m).wait()
    right_parts(2, 4)
    join_parts(0)

    far_xm.wait_recv()
    x_z3 = hand(pos(2, zl, c), z_dev, 2, 2)
    z_xp.wait_recv()
    zfar_xp = hand(pos(-1, zo, c), xp_dev, 0, 1)
    z_xm1.wait_recv()
    zfar_xm = hand(pos(1, zo, c), xm_dev, 1, 1)
    x_z1.wait_recv()
    sib_2 = [hand(pos(-1, zo, c), sibling, 0, 2), hand(pos(1, zo, c), sibling, 2, 2)]
    hop0 = ring_hop(0, 0, 1, zo)
    dir0 = ring_direct(0, 0, 1, zo)

    group0 = [(1, zl), (-1, zl), (0, zl)]
    await_all(sib_0)
    await_all(sib_1)
    left_both(group0)

    far_xp.wait_recv()
    sib_far = hand(pos(2, zl, c), sibling)
    z_xm0.wait_recv()
    x_z2.wait_recv()
    sib_2 += [hand(pos(1, zo, c), sibling, 0, 2), hand(pos(-1, zo, c), sibling, 2, 2)]

    first_of(group0)
    join_parts(2)
    hop2 = ring_hop(2, 2, 3, zo)
    dir2 = ring_direct(2, 2, 3, zo)
    hop1 = ring_hop(1, 0, 1, zl)
    hop3 = ring_hop(3, 2, 3, zl)

    zfar_xp.wait_recv()
    zfar_xm.wait_recv()
    x_z3.wait_recv()
    sib_2.append(hand(pos(2, zo, c), sibling))

    group1 = [(2, zl), (0, zo)]
    sib_far.wait_recv()
    left_both(group1)
    first_of(group1)
    acc0 = ring_second(0, 0, 1, zo, hop0)
    acc2 = ring_second(2, 2, 3, zo, hop2)
    dir1 = ring_direct(1, 0, 1, zl)
    dir3 = ring_direct(3, 2, 3, zl)

    group2 = [(2, zo), (1, zo), (-1, zo)]
    await_all(sib_2)
    left_both(group2)
    first_of(group2)
    correlate(group0)
    second_of(group0)
    acc1 = ring_second(1, 0, 1, zl, hop1)
    acc3 = ring_second(3, 2, 3, zl, hop3)
    correlate(group1)
    correlate(group2)

    def pairs():
        for m in range(2):

            def step(p, acc, m=m):
                return acc + fold(lg[p, 2 * c + m].astype(F32) * r[m, p].astype(F32))

            sums[1] += lax.fori_loop(0, 16, step, jnp.zeros((8, 128), F32))

    pl.when(blk // 2 == grp)(pairs)
    sum_copy = send(sums.at[pl.ds(0, 2)], sums.at[pl.ds(2, 2)], sibling)

    second_of(group1)

    sum_copy.wait_recv()
    sums[4:6] = sums[0:2] + sums[2:4]
    sum_copy = send(sums.at[pl.ds(4, 2)], sums.at[pl.ds(6, 2)], z_dev)

    ring_third(0, 0, 1, zo, dir0, acc0)
    z_got0 = z_send(0, 0, 1)
    ring_third(2, 2, 3, zo, dir2, acc2)
    z_got1 = z_send(1, 2, 3)

    second_of(group2)

    sum_copy.wait_recv()
    sums[8:10] = sums[4:6] + sums[6:8]
    sum_copy = send(sums.at[pl.ds(8, 2)], sums.at[pl.ds(10, 2)], h_dev)

    own = (y + 4 - x) % 4

    def y_total(z, core):
        for side in range(2):
            for m in range(2):
                for copy in to_owner(0, z, m, core, side, y_devs[0]):
                    copy.wait_recv()

        def step(m, carry):
            at = sl.at[own, z, m, core]
            decode_add(at, at, [(yr.at[i, z, m, core], ysr.at[i, z, m, core]) for i in range(2)])
            return carry

        lax.fori_loop(0, 2, step, 0)

    sum_copy.wait_recv()
    xs[x] = sums[8:10] + sums[10:12]
    x_sums = [send(xs.at[x], xs.at[x], device) for device in (xp_dev, xm_dev, x2_dev)]

    h_got = []
    for core in range(2):
        y_total(1 - zh, core)

        def h_encode(m, carry, core=core):
            encode(sl.at[own, 1 - zh, m, core], hs.at[core, m], hss.at[core, m])
            return carry

        lax.fori_loop(0, 2, h_encode, 0)
        h_got.append(
            [send(hs.at[core], hr.at[core], h_dev), send(hss.at[core], hsr.at[core], h_dev)]
        )

    ring_third(1, 0, 1, zl, dir1, acc1)
    ring_third(3, 2, 3, zl, dir3, acc3)

    await_all(x_sums)
    ysum[y] = xs[0] + xs[1] + xs[2] + xs[3]
    y_sums = [send(ysum.at[y], ysum.at[y], device) for device in y_devs]

    z_take(0, 0, 1, z_got0)
    z_take(1, 2, 3, z_got1)
    sr_copies = []
    for j in range(4):
        copy = pltpu.make_async_copy(tot.at[j, xz(0, zl)], sr_out.at[:, j], load_sem.at[j])
        copy.start()
        sr_copies.append(copy)

    for core in range(2):
        y_total(zh, core)

    await_all(y_sums)
    both = ysum[0] + ysum[1] + ysum[2] + ysum[3]
    numerator = jnp.sum(jnp.sum(both[0], axis=0, keepdims=True), axis=1, keepdims=True)
    denominator = jnp.sum(jnp.sum(both[1], axis=0, keepdims=True), axis=1, keepdims=True)
    ray[0] = (numerator / denominator)[0, 0]
    ray_copy = pltpu.make_async_copy(ray, ray_out, load_sem.at[8])
    ray_copy.start()

    sl_copies = []
    for core in range(2):
        await_all(h_got[core])
        for m in range(2):
            keep = screen_ref[0, 2 * blk + m].astype(F32)
            at = sl.at[own, zh, m, core]
            decode_add(at, at, [(hr.at[core, m], hsr.at[core, m])], keep)
            copy = pltpu.make_async_copy(
                at, sl_out.at[pl.ds(core * 48, 48), m], load_sem.at[4 + m * 2 + core]
            )
            copy.start()
            sl_copies.append(copy)
    for copy in sr_copies + sl_copies + [ray_copy]:
        copy.wait()

    def drain():
        for copy in started:
            copy.wait_send()
        for j in range(4):
            part_copy(j).wait_send()
        for dx, z in group0 + group1 + group2:
            y_drain(dx, z)

    drain()


def hand_out(sr_ref, sl_ref, sr_out, sl_out, sr_block, sl_block, sems):
    into = [
        pltpu.make_async_copy(sr_ref, sr_block, sems.at[0]),
        pltpu.make_async_copy(sl_ref, sl_block, sems.at[1]),
    ]
    out = [
        pltpu.make_async_copy(sr_block, sr_out, sems.at[2]),
        pltpu.make_async_copy(sl_block, sl_out, sems.at[3]),
    ]
    for copy in into:
        copy.start()
    for first, second in zip(into, out):
        first.wait()
        second.start()
    for copy in out:
        copy.wait()


def body(right_vector, left_vector, cycle_weights, screen):
    right = right_vector.reshape(768, 2, 768)
    left = left_vector.reshape(48, 4, 768)
    anywhere = pl.BlockSpec(memory_space=pl.ANY)
    scratch = [
        pltpu.VMEM((2, 4, 768, 768), BF16),
        pltpu.VMEM((768, 2, 768), BF16),
        pltpu.VMEM((48, 4, 768), BF16),
        pltpu.VMEM((2, 16, 48, 768), BF16),
        pltpu.VMEM((2, 16, 48, 768), BF16),
        pltpu.VMEM((16, 4, 48, 768), BF16),
        pltpu.VMEM((4, 8, 2, 48, 768), F32),
        pltpu.VMEM((4, 8, 48, 768), F32),
        pltpu.VMEM((4, 2, 2, 2, 48, 768), F32),
        pltpu.VMEM((4, 6, 48, 768), I16),
        pltpu.VMEM((4, 6, 48, 768), I16),
        pltpu.VMEM((4, 6, 8, 128), F32),
        pltpu.VMEM((4, 6, 8, 128), F32),
        pltpu.VMEM((2, 2, 48, 768), I16),
        pltpu.VMEM((2, 2, 48, 768), I16),
        pltpu.VMEM((2, 2, 8, 128), F32),
        pltpu.VMEM((2, 2, 8, 128), F32),
        pltpu.VMEM((4, 2, 2, 2, 48, 768), I16),
        pltpu.VMEM((2, 2, 2, 2, 48, 768), I16),
        pltpu.VMEM((2, 2, 2, 48, 768), I16),
        pltpu.VMEM((4, 2, 2, 2, 8, 128), F32),
        pltpu.VMEM((2, 2, 2, 2, 8, 128), F32),
        pltpu.VMEM((2, 2, 2, 8, 128), F32),
        pltpu.VMEM((2, 2, 48, 768), I16),
        pltpu.VMEM((2, 2, 48, 768), I16),
        pltpu.VMEM((2, 2, 8, 128), F32),
        pltpu.VMEM((2, 2, 8, 128), F32),
        pltpu.VMEM((12, 8, 128), F32),
        pltpu.VMEM((4, 2, 8, 128), F32),
        pltpu.VMEM((4, 2, 8, 128), F32),
        pltpu.SMEM((1,), F32),
        pltpu.SemaphoreType.DMA((10,)),
        pltpu.SemaphoreType.DMA((N_SEM,)),
        pltpu.SemaphoreType.DMA((N_SEM,)),
        pltpu.SemaphoreType.DMA((4, 2, 2, 2, 2)),
        pltpu.SemaphoreType.DMA((2, 2, 2, 2, 2)),
        pltpu.SemaphoreType.DMA((2, 2, 2, 2)),
        pltpu.SemaphoreType.DMA((4, 2)),
    ]
    sr, sl, ray = pl.pallas_call(
        kernel,
        out_shape=(
            jax.ShapeDtypeStruct((48, 4, 768), F32),
            jax.ShapeDtypeStruct((96, 2, 768), F32),
            jax.ShapeDtypeStruct((1,), F32),
        ),
        in_specs=[pl.BlockSpec(memory_space=pltpu.SMEM), anywhere, anywhere, anywhere],
        out_specs=(anywhere, anywhere, anywhere),
        scratch_shapes=scratch,
        compiler_params=pltpu.CompilerParams(
            collective_id=0, has_side_effects=True, vmem_limit_bytes=60 * 2**20
        ),
        cost_estimate=pl.CostEstimate(
            flops=14_500_000_000, bytes_accessed=13_000_000, transcendentals=0
        ),
    )(screen, right, left, cycle_weights)
    sigma_right, sigma_left = pl.pallas_call(
        hand_out,
        out_shape=(jax.ShapeDtypeStruct(sr.shape, F32), jax.ShapeDtypeStruct(sl.shape, F32)),
        in_specs=[anywhere, anywhere],
        out_specs=(anywhere, anywhere),
        scratch_shapes=[
            pltpu.VMEM(sr.shape, F32),
            pltpu.VMEM(sl.shape, F32),
            pltpu.SemaphoreType.DMA((4,)),
        ],
    )(sr, sl)
    return sigma_right[:, None], sigma_left[:, None], ray


def solution(mesh):
    in_specs = (
        P(None, None, "blk", None),
        P("blk", None, "grp", None),
        P("blk", "grp", None, None),
        P(),
    )
    out_specs = (P("blk", None, "grp", None), P("grp", None, "blk", None), P())
    return jax.shard_map(body, mesh=mesh, in_specs=in_specs, out_specs=out_specs, check_vma=False)
```

```python
import functools

import jax
import jax.numpy as jnp
from jax import lax
from jax.experimental import pallas as pl
from jax.experimental.pallas import tpu as pltpu
from jax.sharding import PartitionSpec as P

MESH = pl.DeviceIdType.MESH
F32 = jnp.float32
BF16 = jnp.bfloat16
I16 = jnp.int16
LEVELS = 32000.0
N_SEM = 94


def dot_nn(a, b):
    return jnp.dot(a, b, preferred_element_type=F32)


def dot_nt(a, b):
    return lax.dot_general(a, b, (((1,), (1,)), ((), ())), preferred_element_type=F32)


def wide(scale):
    return jnp.concatenate([scale] * 6, axis=1)


def band(i):
    return pl.ds(pl.multiple_of(i * 16, 16), 16)


def encode(src, q_ref, scale_ref):
    def top_step(i, top):
        return jnp.maximum(top, jnp.abs(src[band(i)]))

    top = lax.fori_loop(0, 3, top_step, jnp.full((16, 768), 1e-30, F32))
    top = jnp.max(top, axis=0, keepdims=True)
    top = functools.reduce(jnp.maximum, [top[:, i * 128 : (i + 1) * 128] for i in range(6)])
    inverse = wide(LEVELS / top)
    scale_ref[...] = jnp.broadcast_to(top * (1.0 / LEVELS), (8, 128))

    def step(i, carry):
        q_ref[band(i)] = jnp.round(src[band(i)] * inverse).astype(jnp.int32).astype(I16)
        return carry

    lax.fori_loop(0, 3, step, 0)


def decode_add(dst, src, terms, factor=1.0):
    scales = [wide(scale[0:1]) for _, scale in terms]

    def step(i, carry):
        total = src[band(i)]
        for (q, _), scale in zip(terms, scales):
            total = total + q[band(i)].astype(jnp.int32).astype(F32) * scale
        dst[band(i)] = total * factor
        return carry

    lax.fori_loop(0, 3, step, 0)


def fold(x):
    rows = functools.reduce(jnp.add, [x[i * 8 : (i + 1) * 8] for i in range(6)])
    return functools.reduce(jnp.add, [rows[:, i * 128 : (i + 1) * 128] for i in range(6)])


def kernel(
    screen_ref, right_hbm, left_hbm, weights_hbm, sr_out, sl_out, ray_out,
    w, right_raw, left_raw, r, rs, lg, part, tot, sl,
    ring_s, ring_r, rsc_s, rsc_r,
    zf_s, zf_r, zfs_s, zfs_r,
    ys, yr, yh, yss, ysr, yhs,
    hs, hr, hss, hsr,
    sums, xs, ysum, ray,
    load_sem, send_sem, recv_sem, ysend_sem, yrecv_sem, yhop_sem, part_sem,
):
    blk = lax.axis_index("blk")
    grp = lax.axis_index("grp")
    x, zl, c = blk // 4, (blk // 2) % 2, blk % 2
    y, zh = grp // 2, grp % 2
    zo = 1 - zl
    sibling = (blk + 1 - 2 * c, grp)
    z_dev = (blk + 2 - 4 * zl, grp)
    xp_dev = ((blk + 4) % 16, grp)
    xm_dev = ((blk + 12) % 16, grp)
    x2_dev = ((blk + 8) % 16, grp)
    y_devs = [(blk, (grp + 2 * k) % 8) for k in (1, 2, 3)]
    h_dev = (blk, grp + 1 - 2 * zh)

    loads = []

    def load(src, dst):
        copy = pltpu.make_async_copy(src, dst, load_sem.at[len(loads)])
        copy.start()
        loads.append(copy)
        return copy

    def pos(dx, z, core):
        return ((x + dx) % 4) * 4 + z * 2 + core

    here = pos(0, zl, c)
    left_in = load(left_hbm, left_raw)
    right_in = load(right_hbm, right_raw)

    def weight_copy(j, m):
        return pltpu.make_async_copy(weights_hbm.at[m, j], w.at[m, j], load_sem.at[2 + j * 2 + m])

    for j in range(4):
        for m in range(2):
            weight_copy(j, m).start()

    barrier = pltpu.get_barrier_semaphore()
    partners = [sibling, z_dev, xp_dev, xm_dev, x2_dev, h_dev] + y_devs
    for partner in partners:
        pl.semaphore_signal(barrier, inc=1, device_id=partner, device_id_type=MESH)
    left_in.wait()
    for j in range(4):
        lg[here, j] = left_raw[:, j, :]
    pl.semaphore_wait(barrier, len(partners))

    started = []

    def send(src, dst, device):
        k = len(started)
        copy = pltpu.make_async_remote_copy(
            src_ref=src, dst_ref=dst, send_sem=send_sem.at[k], recv_sem=recv_sem.at[k],
            device_id=device, device_id_type=MESH,
        )
        copy.start()
        started.append(copy)
        return copy

    def hand(p, device, j=0, count=4):
        ref = lg.at[p, pl.ds(j, count)]
        return send(ref, ref, device)

    def await_all(copies):
        for copy in copies:
            copy.wait_recv()

    own_xp = [hand(here, xp_dev, 0, 2), hand(here, xp_dev, 2, 2)]
    own_xm = [hand(here, xm_dev, 2, 2), hand(here, xm_dev, 0, 2)]
    own_z = [hand(here, z_dev, 0, 2), hand(here, z_dev, 2, 2)]
    sib_0 = [hand(here, sibling)]
    sib_1 = []

    def part_copy(j):
        return pltpu.make_async_remote_copy(
            src_ref=part.at[j, :, 1 - c], dst_ref=tot.at[j], send_sem=part_sem.at[j, 0],
            recv_sem=part_sem.at[j, 1], device_id=sibling, device_id_type=MESH,
        )

    def right_parts(first, last):
        def step(j, carry):
            acc = dot_nn(rs[0].reshape(768, 768), w[0, j]) + dot_nn(rs[1].reshape(768, 768), w[1, j])
            part[j] = acc.reshape(8, 2, 48, 768)
            part_copy(j).start()
            return carry

        lax.fori_loop(first, last, step, 0)

    def join_parts(first):
        for j in range(first, first + 2):
            part_copy(j).wait_recv()

        def step(k, carry):
            j, at = first + k // 8, k % 8
            tot[j, at] = tot[j, at] + part[j, at, c]
            return carry

        lax.fori_loop(0, 16, step, 0)

    sums[0:2] = jnp.zeros((2, 8, 128), F32)

    def left_rows(chunks, m):
        rows = [pos(dx, z, core) for dx, z in chunks for core in range(2)]
        acc = None
        for j in range(4):
            block = jnp.concatenate([lg[p, j] for p in rows], axis=0)
            term = dot_nt(block, w[m, j])
            acc = term if acc is None else acc + term
        for i in range(len(rows)):
            dx, z = chunks[i // 2]
            sl[dx % 4, z, m, i % 2] = acc[i * 48 : (i + 1) * 48]

    def left_both(chunks):
        def step(m, carry):
            left_rows(chunks, m)
            return carry

        lax.fori_loop(0, 2, step, 0)

    def correlate(chunks):
        for dx, z in chunks:

            def step(k, acc, dx=dx, z=z):
                m, core = k // 2, k % 2
                return acc + fold(sl[dx % 4, z, m, core] * rs[m, pos(dx, z, core)].astype(F32))

            sums[0] += lax.fori_loop(0, 4, step, jnp.zeros((8, 128), F32))

    def role(dx):
        owner = (x + dx) % 4
        step = (y + 4 - owner) % 4
        return owner, step, step // 2

    def y_copies(dx, z, m, core, dst, dst_scale, sems, device):
        at = (dx % 4, z, m, core)
        return [
            pltpu.make_async_remote_copy(
                src_ref=src.at[at], dst_ref=to, send_sem=ysend_sem.at[at + (i,)], recv_sem=sems.at[i],
                device_id=device, device_id_type=MESH,
            )
            for i, (src, to) in enumerate(((ys, dst), (yss, dst_scale)))
        ]

    def to_owner(dx, z, m, core, side, device):
        at = (side, z, m, core)
        return y_copies(dx, z, m, core, yr.at[at], ysr.at[at], yrecv_sem.at[at], device)

    def to_side(dx, z, m, core, device):
        at = (z, m, core)
        return y_copies(dx, z, m, core, yh.at[at], yhs.at[at], yhop_sem.at[at], device)

    def y_encode(d, z, m, core):
        encode(sl.at[d, z, m, core], ys.at[d, z, m, core], yss.at[d, z, m, core])

    def y_far(dx, z):
        owner, step, side = role(dx)

        def far():
            for m in range(2):

                def piece(core, carry, m=m):
                    y_encode(dx % 4, z, m, core)
                    for copy in to_side(dx, z, m, core, y_devs[2 * m]):
                        copy.start()
                    return carry

                lax.fori_loop(0, 2, piece, 0)

        pl.when(step == 2)(far)

    def y_near(dx, z):
        owner, step, side = role(dx)

        def near():
            def piece(core, carry):
                y_encode(dx % 4, z, side, core)
                for copy in to_owner(dx, z, side, core, side, (blk, owner * 2 + zh)):
                    copy.start()
                return carry

            lax.fori_loop(0, 2, piece, 0)

        pl.when(step % 2 == 1)(near)

    def y_second(dx, z, core):
        owner, step, side = role(dx)
        d = dx % 4
        other = 1 - side

        def near():
            for copy in to_side(dx, z, other, core, y_devs[0]):
                copy.wait_recv()
            at = sl.at[d, z, other, core]
            decode_add(at, at, [(yh.at[z, other, core], yhs.at[z, other, core])])
            y_encode(d, z, other, core)
            for copy in to_owner(dx, z, other, core, side, (blk, owner * 2 + zh)):
                copy.start()

        pl.when(step % 2 == 1)(near)

    def y_drain(dx, z):
        owner, step, side = role(dx)

        def done():
            def piece(k, carry):
                for copy in to_side(dx, z, k // 2, k % 2, y_devs[0]):
                    copy.wait_send()
                return carry

            lax.fori_loop(0, 4, piece, 0)

        pl.when(step != 0)(done)

    def first_of(chunks):
        for dx, z in chunks:
            y_far(dx, z)
        for dx, z in chunks:
            y_near(dx, z)

    def second_of(chunks):
        for core in range(2):
            for dx, z in chunks:
                y_second(dx, z, core)

    def ring_send(n, kind, block, device):
        encode(block, ring_s.at[n, kind], rsc_s.at[n, kind])
        return [
            send(ring_s.at[n, kind], ring_r.at[n, kind], device),
            send(rsc_s.at[n, kind], rsc_r.at[n, kind], device),
        ]

    def ring_add(n, at, kinds):
        for _, copies in kinds:
            await_all(copies)
        decode_add(at, at, [(ring_r.at[n, kind], rsc_r.at[n, kind]) for kind, _ in kinds])

    def xz(dx, z):
        return ((x + dx) % 4) * 2 + z

    def ring_hop(n, ja, jb, z):
        hop_p = ring_send(n, 0, tot.at[ja, xz(2, z)], xp_dev)
        hop_m = ring_send(n, 1, tot.at[jb, xz(2, z)], xm_dev)
        return hop_p, hop_m

    def ring_direct(n, ja, jb, z):
        dir_p = ring_send(n, 2, tot.at[jb, xz(1, z)], xp_dev)
        dir_m = ring_send(n, 3, tot.at[ja, xz(-1, z)], xm_dev)
        return dir_p, dir_m

    def ring_second(n, ja, jb, z, hop):
        to_p, to_m = tot.at[ja, xz(1, z)], tot.at[jb, xz(-1, z)]
        ring_add(n, to_p, [(0, hop[0])])
        acc_p = ring_send(n, 4, to_p, xp_dev)
        ring_add(n, to_m, [(1, hop[1])])
        acc_m = ring_send(n, 5, to_m, xm_dev)
        return acc_p, acc_m

    def ring_third(n, ja, jb, z, direct, second):
        at = xz(0, z)
        ring_add(n, tot.at[ja, at], [(3, direct[1]), (4, second[0])])
        ring_add(n, tot.at[jb, at], [(2, direct[0]), (5, second[1])])

    def z_send(n, ja, jb):
        for i, j in enumerate((ja, jb)):
            encode(tot.at[j, xz(0, zo)], zf_s.at[n, i], zfs_s.at[n, i])
        return [send(zf_s.at[n], zf_r.at[n], z_dev), send(zfs_s.at[n], zfs_r.at[n], z_dev)]

    def z_take(n, ja, jb, copies):
        await_all(copies)
        for i, j in enumerate((ja, jb)):
            at = tot.at[j, xz(0, zl)]
            decode_add(at, at, [(zf_r.at[n, i], zfs_r.at[n, i])])

    right_in.wait()
    for m in range(2):

        def right_rows(k, carry, m=m):
            r[m, k] = right_raw[pl.ds(pl.multiple_of(k * 48, 48), 48), m, :]
            return carry

        lax.fori_loop(0, 16, right_rows, 0)

    own_z[0].wait_recv()
    z_xp = hand(pos(0, zo, c), xp_dev, 0, 2)
    own_xp[0].wait_recv()
    far_xp = hand(pos(-1, zl, c), xp_dev, 0, 2)
    own_xm[0].wait_recv()
    far_xm = hand(pos(1, zl, c), xm_dev, 2, 2)
    z_xm1 = hand(pos(0, zo, c), xm_dev, 1, 1)
    z_xm0 = hand(pos(0, zo, c), xm_dev, 0, 1)
    x_z1 = hand(pos(1, zl, c), z_dev, 2, 2)
    sib_1 += [hand(pos(0, zo, c), sibling, 0, 2), hand(pos(-1, zl, c), sibling, 0, 2)]
    sib_1 += [hand(pos(1, zl, c), sibling, 2, 2)]

    for m in range(2):
        keep = screen_ref[0, 2 * blk + m].astype(F32).astype(BF16)

        def screen_rows(k, carry, m=m, keep=keep):
            rs[m, k] = r[m, k] * keep
            return carry

        lax.fori_loop(0, 16, screen_rows, 0)
    for j in (0, 1):
        for m in range(2):
            weight_copy(j, m).wait()
    right_parts(0, 2)

    own_xp[1].wait_recv()
    x_z2 = hand(pos(-1, zl, c), z_dev, 2, 2)
    own_xm[1].wait_recv()
    own_z[1].wait_recv()
    sib_1 += [hand(pos(0, zo, c), sibling, 2, 2), hand(pos(-1, zl, c), sibling, 2, 2)]
    sib_1 += [hand(pos(1, zl, c), sibling, 0, 2)]

    for j in (2, 3):
        for m in range(2):
            weight_copy(j, m).wait()
    right_parts(2, 4)
    join_parts(0)

    far_xm.wait_recv()
    x_z3 = hand(pos(2, zl, c), z_dev, 2, 2)
    z_xp.wait_recv()
    zfar_xp = hand(pos(-1, zo, c), xp_dev, 0, 1)
    z_xm1.wait_recv()
    zfar_xm = hand(pos(1, zo, c), xm_dev, 1, 1)
    x_z1.wait_recv()
    sib_2 = [hand(pos(-1, zo, c), sibling, 0, 2), hand(pos(1, zo, c), sibling, 2, 2)]
    hop0 = ring_hop(0, 0, 1, zo)
    dir0 = ring_direct(0, 0, 1, zo)

    group0 = [(1, zl), (-1, zl), (0, zl)]
    await_all(sib_0)
    await_all(sib_1)
    left_both(group0)

    far_xp.wait_recv()
    sib_far = hand(pos(2, zl, c), sibling)
    z_xm0.wait_recv()
    x_z2.wait_recv()
    sib_2 += [hand(pos(1, zo, c), sibling, 0, 2), hand(pos(-1, zo, c), sibling, 2, 2)]

    first_of(group0)
    join_parts(2)
    hop2 = ring_hop(2, 2, 3, zo)
    dir2 = ring_direct(2, 2, 3, zo)
    hop1 = ring_hop(1, 0, 1, zl)
    hop3 = ring_hop(3, 2, 3, zl)

    zfar_xp.wait_recv()
    zfar_xm.wait_recv()
    x_z3.wait_recv()
    sib_2.append(hand(pos(2, zo, c), sibling))

    group1 = [(2, zl), (0, zo)]
    sib_far.wait_recv()
    left_both(group1)
    first_of(group1)
    acc0 = ring_second(0, 0, 1, zo, hop0)
    acc2 = ring_second(2, 2, 3, zo, hop2)
    dir1 = ring_direct(1, 0, 1, zl)
    dir3 = ring_direct(3, 2, 3, zl)

    group2 = [(2, zo), (1, zo), (-1, zo)]
    await_all(sib_2)
    left_both(group2)
    first_of(group2)
    correlate(group0)
    second_of(group0)
    acc1 = ring_second(1, 0, 1, zl, hop1)
    acc3 = ring_second(3, 2, 3, zl, hop3)
    correlate(group1)
    correlate(group2)

    def pairs():
        for m in range(2):

            def step(p, acc, m=m):
                return acc + fold(lg[p, 2 * c + m].astype(F32) * r[m, p].astype(F32))

            sums[1] += lax.fori_loop(0, 16, step, jnp.zeros((8, 128), F32))

    pl.when(blk // 2 == grp)(pairs)
    sum_copy = send(sums.at[pl.ds(0, 2)], sums.at[pl.ds(2, 2)], sibling)

    second_of(group1)

    sum_copy.wait_recv()
    sums[4:6] = sums[0:2] + sums[2:4]
    sum_copy = send(sums.at[pl.ds(4, 2)], sums.at[pl.ds(6, 2)], z_dev)

    ring_third(0, 0, 1, zo, dir0, acc0)
    z_got0 = z_send(0, 0, 1)
    ring_third(2, 2, 3, zo, dir2, acc2)
    z_got1 = z_send(1, 2, 3)

    second_of(group2)

    sum_copy.wait_recv()
    sums[8:10] = sums[4:6] + sums[6:8]
    sum_copy = send(sums.at[pl.ds(8, 2)], sums.at[pl.ds(10, 2)], h_dev)

    own = (y + 4 - x) % 4

    def y_total(z, core):
        for side in range(2):
            for m in range(2):
                for copy in to_owner(0, z, m, core, side, y_devs[0]):
                    copy.wait_recv()

        def step(m, carry):
            at = sl.at[own, z, m, core]
            decode_add(at, at, [(yr.at[i, z, m, core], ysr.at[i, z, m, core]) for i in range(2)])
            return carry

        lax.fori_loop(0, 2, step, 0)

    sum_copy.wait_recv()
    xs[x] = sums[8:10] + sums[10:12]
    x_sums = [send(xs.at[x], xs.at[x], device) for device in (xp_dev, xm_dev, x2_dev)]

    h_got = []
    for core in range(2):
        y_total(1 - zh, core)

        def h_encode(m, carry, core=core):
            encode(sl.at[own, 1 - zh, m, core], hs.at[core, m], hss.at[core, m])
            return carry

        lax.fori_loop(0, 2, h_encode, 0)
        h_got.append(
            [send(hs.at[core], hr.at[core], h_dev), send(hss.at[core], hsr.at[core], h_dev)]
        )
        if core == 0:
            await_all(x_sums)
            ysum[y] = xs[0] + xs[1] + xs[2] + xs[3]
            y_sums = [send(ysum.at[y], ysum.at[y], device) for device in y_devs]

    ring_third(1, 0, 1, zl, dir1, acc1)
    ring_third(3, 2, 3, zl, dir3, acc3)

    z_take(0, 0, 1, z_got0)
    z_take(1, 2, 3, z_got1)
    sr_copies = []
    for j in range(4):
        copy = pltpu.make_async_copy(tot.at[j, xz(0, zl)], sr_out.at[:, j], load_sem.at[j])
        copy.start()
        sr_copies.append(copy)

    for core in range(2):
        y_total(zh, core)

    await_all(y_sums)
    both = ysum[0] + ysum[1] + ysum[2] + ysum[3]
    numerator = jnp.sum(jnp.sum(both[0], axis=0, keepdims=True), axis=1, keepdims=True)
    denominator = jnp.sum(jnp.sum(both[1], axis=0, keepdims=True), axis=1, keepdims=True)
    ray[0] = (numerator / denominator)[0, 0]
    ray_copy = pltpu.make_async_copy(ray, ray_out, load_sem.at[8])
    ray_copy.start()

    sl_copies = []
    for core in range(2):
        await_all(h_got[core])
        for m in range(2):
            keep = screen_ref[0, 2 * blk + m].astype(F32)
            at = sl.at[own, zh, m, core]
            decode_add(at, at, [(hr.at[core, m], hsr.at[core, m])], keep)
            copy = pltpu.make_async_copy(
                at, sl_out.at[pl.ds(core * 48, 48), m], load_sem.at[4 + m * 2 + core]
            )
            copy.start()
            sl_copies.append(copy)
    for copy in sr_copies + sl_copies + [ray_copy]:
        copy.wait()

    def drain():
        for copy in started:
            copy.wait_send()
        for j in range(4):
            part_copy(j).wait_send()
        for dx, z in group0 + group1 + group2:
            y_drain(dx, z)

    drain()


def hand_out(sr_ref, sl_ref, sr_out, sl_out, sr_block, sl_block, sems):
    into = [
        pltpu.make_async_copy(sr_ref, sr_block, sems.at[0]),
        pltpu.make_async_copy(sl_ref, sl_block, sems.at[1]),
    ]
    out = [
        pltpu.make_async_copy(sr_block, sr_out, sems.at[2]),
        pltpu.make_async_copy(sl_block, sl_out, sems.at[3]),
    ]
    for copy in into:
        copy.start()
    for first, second in zip(into, out):
        first.wait()
        second.start()
    for copy in out:
        copy.wait()


def body(right_vector, left_vector, cycle_weights, screen):
    right = right_vector.reshape(768, 2, 768)
    left = left_vector.reshape(48, 4, 768)
    anywhere = pl.BlockSpec(memory_space=pl.ANY)
    scratch = [
        pltpu.VMEM((2, 4, 768, 768), BF16),
        pltpu.VMEM((768, 2, 768), BF16),
        pltpu.VMEM((48, 4, 768), BF16),
        pltpu.VMEM((2, 16, 48, 768), BF16),
        pltpu.VMEM((2, 16, 48, 768), BF16),
        pltpu.VMEM((16, 4, 48, 768), BF16),
        pltpu.VMEM((4, 8, 2, 48, 768), F32),
        pltpu.VMEM((4, 8, 48, 768), F32),
        pltpu.VMEM((4, 2, 2, 2, 48, 768), F32),
        pltpu.VMEM((4, 6, 48, 768), I16),
        pltpu.VMEM((4, 6, 48, 768), I16),
        pltpu.VMEM((4, 6, 8, 128), F32),
        pltpu.VMEM((4, 6, 8, 128), F32),
        pltpu.VMEM((2, 2, 48, 768), I16),
        pltpu.VMEM((2, 2, 48, 768), I16),
        pltpu.VMEM((2, 2, 8, 128), F32),
        pltpu.VMEM((2, 2, 8, 128), F32),
        pltpu.VMEM((4, 2, 2, 2, 48, 768), I16),
        pltpu.VMEM((2, 2, 2, 2, 48, 768), I16),
        pltpu.VMEM((2, 2, 2, 48, 768), I16),
        pltpu.VMEM((4, 2, 2, 2, 8, 128), F32),
        pltpu.VMEM((2, 2, 2, 2, 8, 128), F32),
        pltpu.VMEM((2, 2, 2, 8, 128), F32),
        pltpu.VMEM((2, 2, 48, 768), I16),
        pltpu.VMEM((2, 2, 48, 768), I16),
        pltpu.VMEM((2, 2, 8, 128), F32),
        pltpu.VMEM((2, 2, 8, 128), F32),
        pltpu.VMEM((12, 8, 128), F32),
        pltpu.VMEM((4, 2, 8, 128), F32),
        pltpu.VMEM((4, 2, 8, 128), F32),
        pltpu.SMEM((1,), F32),
        pltpu.SemaphoreType.DMA((10,)),
        pltpu.SemaphoreType.DMA((N_SEM,)),
        pltpu.SemaphoreType.DMA((N_SEM,)),
        pltpu.SemaphoreType.DMA((4, 2, 2, 2, 2)),
        pltpu.SemaphoreType.DMA((2, 2, 2, 2, 2)),
        pltpu.SemaphoreType.DMA((2, 2, 2, 2)),
        pltpu.SemaphoreType.DMA((4, 2)),
    ]
    sr, sl, ray = pl.pallas_call(
        kernel,
        out_shape=(
            jax.ShapeDtypeStruct((48, 4, 768), F32),
            jax.ShapeDtypeStruct((96, 2, 768), F32),
            jax.ShapeDtypeStruct((1,), F32),
        ),
        in_specs=[pl.BlockSpec(memory_space=pltpu.SMEM), anywhere, anywhere, anywhere],
        out_specs=(anywhere, anywhere, anywhere),
        scratch_shapes=scratch,
        compiler_params=pltpu.CompilerParams(
            collective_id=0, has_side_effects=True, vmem_limit_bytes=60 * 2**20
        ),
        cost_estimate=pl.CostEstimate(
            flops=14_500_000_000, bytes_accessed=13_000_000, transcendentals=0
        ),
    )(screen, right, left, cycle_weights)
    sigma_right, sigma_left = pl.pallas_call(
        hand_out,
        out_shape=(jax.ShapeDtypeStruct(sr.shape, F32), jax.ShapeDtypeStruct(sl.shape, F32)),
        in_specs=[anywhere, anywhere],
        out_specs=(anywhere, anywhere),
        scratch_shapes=[
            pltpu.VMEM(sr.shape, F32),
            pltpu.VMEM(sl.shape, F32),
            pltpu.SemaphoreType.DMA((4,)),
        ],
    )(sr, sl)
    return sigma_right[:, None], sigma_left[:, None], ray


def solution(mesh):
    in_specs = (
        P(None, None, "blk", None),
        P("blk", None, "grp", None),
        P("blk", "grp", None, None),
        P(),
    )
    out_specs = (P("blk", None, "grp", None), P("grp", None, "blk", None), P())
    return jax.shard_map(body, mesh=mesh, in_specs=in_specs, out_specs=out_specs, check_vma=False)
```
